128 devices in a mesh: node: 8 (over x, z_lo), wide: 16 (over z_hi, y, core).
Axes of the slice: x: 4, y: 4, z: 4 (z_hi: 2, z_lo: 2; z = z_hi * 2 + z_lo), core: 2. Of those that a mesh axis runs over, the one named last changes fastest.
Arguments:
- grad_codes: int32 [16384, 12288], P(('node', 'wide')), may hold values from -8 to 7
- code_scales: float32 [16384, 96], P(('node', 'wide')), may hold values from 0.01 to 0.1
- requant_scales: int32 [8, 16, 16, 96], P('node', 'wide'), may hold values from 2 to 16
- params: float32 [128, 12288], P(('node', 'wide')), may hold values from -4 to 4
- first_moment: float32 [128, 12288], P(('node', 'wide')), may hold values from -3 to 3
- second_moment: float32 [128, 12288], P(('node', 'wide')), may hold values from 0.1 to 2
- step_count: int32 [1], replicated, may hold values from 1 to 32
Outputs:
- update: float32 [128, 12288], P(('node', 'wide'))
- new_first: float32 [128, 12288], P(('node', 'wide'))
- new_second: float32 [128, 12288], P(('node', 'wide'))
The draws below stay inside these ranges and needn't reach their ends.
Inputs may be any that keep to these rules, and one draw needn't show every extreme that they name: `grad_codes`: 4-bit codes.
All inputs are finite; a program needn't handle non-finite values.
Results may differ from the reference program's by a relative error of at most 0.0035.
Values may be sent and summed in bfloat16 or wider, within the bound.
No kernel may reach another device: no remote copies, remote signals or barrier semaphores. Data moves between devices by JAX's collectives and lax.ppermute only.
A program may use at most 64 MiB of HBM per device.

```python
import math
import jax
import jax.numpy as jnp
from jax import lax

D = 12288
ROWS = 128
N_NODE = 8
N_WIDE = 16
DEVICES = 128


def touch_ends(drawn, stream_key, least, largest):
    spot = [jax.random.randint(jax.random.fold_in(stream_key, axis), (), 0, length) for axis, length in enumerate(drawn.shape)]
    main_axis = drawn.shape.index(max(drawn.shape))
    next_to = spot[:main_axis] + [(spot[main_axis] + 1) % drawn.shape[main_axis]] + spot[main_axis + 1:]
    return drawn.at[tuple(spot)].set(least).at[tuple(next_to)].set(largest)


def levels(own_key, dims, shards, smallest, high):
    loudness = 1.0
    for axis_at, shards_of in shards:
        heights = jax.random.uniform(jax.random.fold_in(jax.random.fold_in(own_key, 6), axis_at), (shards_of,), jnp.float32, smallest / len(shards), high / len(shards))
        loudness = loudness * jnp.repeat(jnp.exp(heights), dims[axis_at] // shards_of).reshape((-1,) + (1,) * (len(dims) - 1 - axis_at))
    return loudness


def scatter_about(key, dims, deviation, limit, cuts=(), kind=jnp.bfloat16):
    factor_of = levels(key, dims, cuts, -0.22, 0.18) if cuts else 1.0
    result = jax.random.normal(key, dims, jnp.float32) * deviation * factor_of
    return jnp.minimum(jnp.maximum(result, -limit), limit).astype(kind)


def setup_inputs(seed: int = 0) -> dict:
    streams_of = jax.random.split(jax.random.key(seed), 8)
    grad_codes = touch_ends(jax.random.randint(streams_of[0], (DEVICES * ROWS, D), -8, 8), jax.random.fold_in(streams_of[0], 1), -8, 7).astype(jnp.int32)
    code_scales = jnp.clip(jnp.exp(math.log(0.1) - 2.3025851 * jax.random.uniform(streams_of[1], (DEVICES * ROWS, D // 128), jnp.float32) ** levels(streams_of[1], (DEVICES * ROWS, D // 128), ((0, 128),), -0.2, 0.2)), 0.01, 0.1)
    requant_scales = touch_ends(jax.random.randint(streams_of[2], (N_NODE, N_WIDE, ROWS // N_NODE, D // 128), 2, 17), jax.random.fold_in(streams_of[2], 1), 2, 16).astype(jnp.int32)
    params = scatter_about(streams_of[3], (ROWS, D), 1.0, 4.0, ((0, 128),), jnp.float32)
    first_moment = scatter_about(streams_of[4], (ROWS, D), 0.5, 3.0, ((0, 128),), jnp.float32)
    second_moment = jnp.clip(jnp.exp(math.log(2.0) - 2.9957323 * jax.random.uniform(streams_of[5], (ROWS, D), jnp.float32) ** levels(streams_of[5], (ROWS, D), ((0, 128),), -0.2, 0.2)), 0.1, 2.0)
    step_count = jax.random.randint(streams_of[6], (1,), 1, 33).astype(jnp.int32)
    return dict(grad_codes=grad_codes, code_scales=code_scales, requant_scales=requant_scales, params=params, first_moment=first_moment, second_moment=second_moment, step_count=step_count)


decay_first = 0.9
decay_second = 0.95
epsilon = 1e-08
weight_decay = 0.1

def dequantize(codes, scales):
    row_count = codes.shape[0]
    blocks = scales.shape[1]
    values = (codes.astype(jnp.float32) + 0.5).reshape(row_count, blocks, 128) * scales[:, :, None]
    return values.reshape(row_count, blocks * 128).astype(jnp.bfloat16)

def requantize(partial_value, scale_two):
    shaped = partial_value.reshape(partial_value.shape[:-1] + (scale_two.shape[-1], 128))
    return jnp.clip(shaped / scale_two[..., None], -8.0, 8.0).astype(jnp.bfloat16)

def restore(requant, scale_two):
    return requant.astype(jnp.float32) * scale_two[..., None]

def adamw(gradient, params, first_moment, second_moment, step_count):
    steps = step_count[0].astype(jnp.float32)
    first = decay_first * first_moment + (1.0 - decay_first) * gradient
    second = decay_second * second_moment + (1.0 - decay_second) * gradient * gradient
    bias_first = 1.0 - jnp.power(jnp.float32(decay_first), steps)
    bias_second = 1.0 - jnp.power(jnp.float32(decay_second), steps)
    update = first / bias_first / (jnp.sqrt(second / bias_second) + epsilon) + weight_decay * params
    return (update, first, second)

def reference(grad_codes, code_scales, requant_scales, params, first_moment, second_moment, step_count):
    codes_view = grad_codes.reshape(N_NODE, N_WIDE, ROWS, D)
    scales_view = code_scales.reshape(N_NODE, N_WIDE, ROWS, D // 128)

    def group_term(total, wide_index):

        def add_device(node_index, partial_value):
            codes_block = codes_view[node_index, wide_index]
            scales_block = scales_view[node_index, wide_index]
            return partial_value + dequantize(codes_block, scales_block).astype(jnp.float32)
        partial_value = lax.fori_loop(0, N_NODE, add_device, jnp.zeros((ROWS, D), jnp.float32))
        scale_two = requant_scales[:, wide_index].reshape(ROWS, D // 128).astype(jnp.float32) / 32.0
        term = restore(requantize(partial_value, scale_two), scale_two).reshape(ROWS, D)
        return (total + term, None)
    gradient, _ = lax.scan(group_term, jnp.zeros((ROWS, D), jnp.float32), jnp.arange(N_WIDE, dtype=jnp.int32))
    return adamw(gradient, params, first_moment, second_moment, step_count)
```

```python
import jax
import jax.numpy as jnp
from jax import lax
from jax.experimental import pallas as pl
from jax.experimental.pallas import tpu as pltpu
from jax.sharding import PartitionSpec as P

decay_first = 0.9
decay_second = 0.95
epsilon = 1e-08
weight_decay = 0.1

BLOCKS = 96
LANES = 128
COLUMNS = BLOCKS * LANES
TILE = 16
PIECES = (
    (0, 32, "PQZ", "PQZ"),
    (32, 32, "QZP", "QZP"),
    (64, 32, "ZPQ", "ZPQ"),
)
AXES = ("node", "wide")
VMEM_LIMIT = 32 * 1024 * 1024


def bits(node):
    high = node >> 2
    return {"P": ((node >> 1) & 1) ^ high, "Q": high, "Z": node & 1}


def node_of(label):
    return (label["Q"] << 2) | ((label["P"] ^ label["Q"]) << 1) | label["Z"]


def pairs(dim0, dim1):
    result = []
    for node in range(8):
        for wide in range(16):
            label = bits(node)
            label[dim1 if wide & 1 else dim0] ^= 1
            result.append((node * 16 + wide, node_of(label) * 16 + wide))
    return result


def block_row(piece, relative):
    mine = bits(lax.axis_index("node"))
    core = lax.axis_index("wide") & 1
    label = {}
    for dim in "PQZ":
        flip0 = relative[piece[2].index(dim)]
        flip1 = relative[piece[3].index(dim)]
        label[dim] = mine[dim] ^ (flip0 + core * (flip1 - flip0))
    return pl.multiple_of(node_of(label) * TILE, TILE)


ORDER = ((1, 1), (1, 0), (0, 1), (0, 0))


def dequantize_kernel(parts, codes_ref, scales_ref, *rest):
    outs = rest[: len(parts)]
    scales_buf = rest[len(parts)]
    stage = rest[len(parts) + 1 : -1]
    sem = rest[-1]
    copies = []
    for n, (piece, first) in enumerate(parts):
        for j, tail in enumerate(ORDER):
            row = block_row(piece, (first,) + tail)
            copy = pltpu.make_async_copy(
                codes_ref.at[pl.ds(row, TILE), pl.ds(piece[0] * LANES, piece[1] * LANES)],
                stage[n].at[pl.ds(j * TILE, TILE), :],
                sem.at[n, j],
            )
            copy.start()
            copies.append((n, j, row, copy))
    scales_buf[:, :BLOCKS] = scales_ref[...].T
    for n, j, row, copy in copies:
        piece = parts[n][0]
        scale = scales_buf[pl.ds(row, TILE), :]
        copy.wait()
        for k in range(piece[1]):
            at = piece[0] + k
            codes = stage[n][j * TILE : (j + 1) * TILE, k * LANES : (k + 1) * LANES]
            values = (codes.astype(jnp.float32) + 0.5) * scale[:, at : at + 1]
            outs[n][j * TILE : (j + 1) * TILE, k * LANES : (k + 1) * LANES] = values.astype(jnp.bfloat16)


def dequantize(parts, codes, scales_t):
    shapes = [(4 * TILE, piece[1] * LANES) for piece, _ in parts]
    return pl.pallas_call(
        lambda *refs: dequantize_kernel(parts, *refs),
        out_shape=[jax.ShapeDtypeStruct(s, jnp.bfloat16) for s in shapes],
        in_specs=[pl.BlockSpec(memory_space=pl.ANY), pl.BlockSpec(memory_space=pltpu.VMEM)],
        out_specs=[pl.BlockSpec(memory_space=pltpu.VMEM) for _ in parts],
        scratch_shapes=[pltpu.VMEM((128, LANES), jnp.float32)]
        + [pltpu.VMEM(s, jnp.int32) for s in shapes]
        + [pltpu.SemaphoreType.DMA((len(parts), 4))],
        compiler_params=pltpu.CompilerParams(vmem_limit_bytes=VMEM_LIMIT),
        name="dequantize",
    )(codes, scales_t)


def finish_kernel(requant_ref, *refs):
    count = len(PIECES)
    keeps, firsts, seconds, thirds = (refs[i * count : (i + 1) * count] for i in range(4))
    send_ref, keep_ref, rows = refs[4 * count :]
    numerators = requant_ref[...].astype(jnp.float32)
    scale = numerators * (1.0 / 32.0)
    inverse = 32.0 / numerators
    for n, piece in enumerate(PIECES):
        for k in range(piece[1]):
            cut = pl.ds(k * LANES, LANES)
            at = piece[0] + k
            partial = (
                keeps[n][3 * TILE : 4 * TILE, cut].astype(jnp.float32)
                + firsts[n][3 * TILE : 4 * TILE, cut].astype(jnp.float32)
            ) + (seconds[n][TILE : 2 * TILE, cut].astype(jnp.float32) + thirds[n][:, cut].astype(jnp.float32))
            coded = jnp.clip(partial * inverse[:, at : at + 1], -8.0, 8.0).astype(jnp.bfloat16)
            rows[pl.ds(at, TILE, stride=BLOCKS), :] = coded.astype(jnp.float32) * scale[:, at : at + 1]
    core = lax.axis_index("wide") & 1
    for j in range(8):
        other = pl.multiple_of((2 * j + 1 - core) * BLOCKS, 8)
        own = pl.multiple_of((2 * j + core) * BLOCKS, 8)
        send_ref[j] = rows[pl.ds(other, BLOCKS), :].astype(jnp.bfloat16)
        keep_ref[j] = rows[pl.ds(own, BLOCKS), :]


def finish(requant, keeps, firsts, seconds, thirds):
    vmem = pl.BlockSpec(memory_space=pltpu.VMEM)
    return pl.pallas_call(
        finish_kernel,
        out_shape=[
            jax.ShapeDtypeStruct((8, BLOCKS, LANES), jnp.bfloat16),
            jax.ShapeDtypeStruct((8, BLOCKS, LANES), jnp.float32),
        ],
        in_specs=[vmem] * (1 + 4 * len(PIECES)),
        out_specs=[vmem, vmem],
        scratch_shapes=[pltpu.VMEM((TILE * BLOCKS, LANES), jnp.float32)],
        compiler_params=pltpu.CompilerParams(vmem_limit_bytes=VMEM_LIMIT),
        name="finish",
    )(requant, *keeps, *firsts, *seconds, *thirds)


def adamw_kernel(bias_ref, terms_ref, params_ref, first_ref, second_ref, update_out, first_out, second_out):
    gradient = terms_ref[0].astype(jnp.float32)
    for j in range(1, 8):
        gradient = gradient + terms_ref[j].astype(jnp.float32)
    first = decay_first * first_ref[...] + (1.0 - decay_first) * gradient
    second = decay_second * second_ref[...] + (1.0 - decay_second) * gradient * gradient
    update_out[...] = (
        first / bias_ref[0] / (jnp.sqrt(second / bias_ref[1]) + epsilon) + weight_decay * params_ref[...]
    )
    first_out[...] = first
    second_out[...] = second


def adamw(bias, terms, params, first_moment, second_moment):
    vmem = pl.BlockSpec(memory_space=pltpu.VMEM)
    return pl.pallas_call(
        adamw_kernel,
        out_shape=[jax.ShapeDtypeStruct((BLOCKS, LANES), jnp.float32)] * 3,
        in_specs=[pl.BlockSpec(memory_space=pltpu.SMEM)] + [vmem] * 4,
        out_specs=[vmem] * 3,
        name="adamw",
    )(bias, terms, params, first_moment, second_moment)


def shards(grad_codes, code_scales, requant_scales, params, first_moment, second_moment, step_count):
    scales_t = code_scales.T
    firsts, seconds, thirds = [], [], []
    for piece in PIECES:
        (send,) = dequantize([(piece, 1)], grad_codes, scales_t)
        firsts.append(lax.ppermute(send, AXES, pairs(piece[2][0], piece[3][0])))
    keeps = dequantize([(piece, 0) for piece in PIECES], grad_codes, scales_t)
    for n, piece in enumerate(PIECES):
        send = firsts[n][: 2 * TILE].astype(jnp.float32) + keeps[n][: 2 * TILE].astype(jnp.float32)
        seconds.append(lax.ppermute(send.astype(jnp.bfloat16), AXES, pairs(piece[2][1], piece[3][1])))
    for n, piece in enumerate(PIECES):
        send = (
            firsts[n][2 * TILE : 3 * TILE].astype(jnp.float32)
            + keeps[n][2 * TILE : 3 * TILE].astype(jnp.float32)
            + seconds[n][:TILE].astype(jnp.float32)
        )
        thirds.append(lax.ppermute(send.astype(jnp.bfloat16), AXES, pairs(piece[2][2], piece[3][2])))
    send, keep = finish(requant_scales.reshape(TILE, BLOCKS), keeps, firsts, seconds, thirds)
    other = lax.ppermute(send, "wide", [(b, b ^ 1) for b in range(16)])
    terms = (keep + other.astype(jnp.float32)).astype(jnp.bfloat16)
    groups = [[2 * j + core for j in range(8)] for core in range(2)]
    terms = lax.all_to_all(terms, "wide", 0, 0, tiled=True, axis_index_groups=groups)
    steps = step_count.astype(jnp.float32)
    bias = jnp.concatenate(
        [1.0 - jnp.power(jnp.float32(decay_first), steps), 1.0 - jnp.power(jnp.float32(decay_second), steps)]
    )
    tall = (BLOCKS, LANES)
    outs = adamw(bias, terms, params.reshape(tall), first_moment.reshape(tall), second_moment.reshape(tall))
    return tuple(out.reshape(1, COLUMNS) for out in outs)


def solution(mesh):
    in_specs = (
        P(("node", "wide"), None),
        P(("node", "wide"), None),
        P("node", "wide", None, None),
        P(("node", "wide"), None),
        P(("node", "wide"), None),
        P(("node", "wide"), None),
        P(),
    )
    out_specs = (P(("node", "wide"), None), P(("node", "wide"), None), P(("node", "wide"), None))
    return jax.shard_map(shards, mesh=mesh, in_specs=in_specs, out_specs=out_specs, check_vma=False)
```

```python
import itertools

import jax
import jax.numpy as jnp
from jax import lax
from jax.experimental import pallas as pl
from jax.experimental.pallas import tpu as pltpu
from jax.sharding import PartitionSpec as P

decay_first = 0.9
decay_second = 0.95
epsilon = 1e-08
weight_decay = 0.1

BLOCKS = 96
LANES = 128
COLUMNS = BLOCKS * LANES
TILE = 16
PIECES = (
    (0, 32, "PQZ", "QZP"),
    (32, 32, "QZP", "ZPQ"),
    (64, 32, "ZPQ", "PQZ"),
)
AXES = ("node", "wide")
VMEM_LIMIT = 32 * 1024 * 1024


def bits(node):
    high = node >> 2
    return {"P": ((node >> 1) & 1) ^ high, "Q": high, "Z": node & 1}


def node_of(label):
    return (label["Q"] << 2) | ((label["P"] ^ label["Q"]) << 1) | label["Z"]


def wide_near(wide, relative):
    high, low, core = (wide >> 2) & 1, (wide >> 1) & 1, wide & 1
    first, second, third = (low ^ high) ^ relative[0], high ^ relative[1], (wide >> 3) ^ relative[2]
    return (third << 3) | (second << 2) | ((first ^ second) << 1) | core


def pairs(dim0, dim1):
    result = []
    for node in range(8):
        for wide in range(16):
            label = bits(node)
            label[dim1 if wide & 1 else dim0] ^= 1
            result.append((node * 16 + wide, node_of(label) * 16 + wide))
    return result


def block_row(piece, relative):
    mine = bits(lax.axis_index("node"))
    core = lax.axis_index("wide") & 1
    label = {}
    for dim in "PQZ":
        flip0 = relative[piece[2].index(dim)]
        flip1 = relative[piece[3].index(dim)]
        label[dim] = mine[dim] ^ (flip0 + core * (flip1 - flip0))
    return pl.multiple_of(node_of(label) * TILE, TILE)


ORDER = ((1, 1), (1, 0), (0, 1), (0, 0))


def dequantize_kernel(parts, codes_ref, scales_ref, *rest):
    outs, stage = rest[: len(parts)], rest[len(parts) : 2 * len(parts)]
    scales_buf, scales, sem, scale_sem = rest[2 * len(parts) :]
    scale_copy = pltpu.make_async_copy(scales_ref, scales_buf, scale_sem)
    scale_copy.start()
    copies = []
    for n, (piece, first) in enumerate(parts):
        for j, tail in enumerate(ORDER):
            row = block_row(piece, (first,) + tail)
            copy = pltpu.make_async_copy(
                codes_ref.at[pl.ds(row, TILE), pl.ds(piece[0] * LANES, piece[1] * LANES)],
                stage[n].at[pl.ds(j * TILE, TILE), :],
                sem.at[n, j],
            )
            copy.start()
            copies.append((n, j, row, copy))
    scale_copy.wait()
    scales[:, :BLOCKS] = scales_buf[...].T
    for n, j, row, copy in copies:
        piece = parts[n][0]
        scale = scales[pl.ds(row, TILE), :]
        copy.wait()
        for k in range(piece[1]):
            at = piece[0] + k
            codes = stage[n][j * TILE : (j + 1) * TILE, k * LANES : (k + 1) * LANES]
            values = (codes.astype(jnp.float32) + 0.5) * scale[:, at : at + 1]
            outs[n][j * TILE : (j + 1) * TILE, k * LANES : (k + 1) * LANES] = values.astype(jnp.bfloat16)


def dequantize(parts, codes, scales_t):
    hbm = pl.BlockSpec(memory_space=pltpu.HBM)
    shapes = [(4 * TILE, piece[1] * LANES) for piece, _ in parts]
    return pl.pallas_call(
        lambda *refs: dequantize_kernel(parts, *refs),
        out_shape=[jax.ShapeDtypeStruct(s, jnp.bfloat16) for s in shapes],
        in_specs=[hbm, hbm],
        out_specs=[pl.BlockSpec(memory_space=pltpu.VMEM) for _ in parts],
        scratch_shapes=[pltpu.VMEM(s, jnp.int32) for s in shapes]
        + [
            pltpu.VMEM((BLOCKS, 128), jnp.float32),
            pltpu.VMEM((128, LANES), jnp.float32),
            pltpu.SemaphoreType.DMA((len(parts), 4)),
            pltpu.SemaphoreType.DMA,
        ],
        compiler_params=pltpu.CompilerParams(vmem_limit_bytes=VMEM_LIMIT),
        name="dequantize",
    )(codes, scales_t)


def finish_kernel(requant_ref, *refs):
    count = len(PIECES)
    keeps, firsts, seconds, thirds = (refs[i * count : (i + 1) * count] for i in range(4))
    send_ref, keep_ref, rows = refs[4 * count :]
    numerators = requant_ref[...].astype(jnp.float32)
    scale = numerators * (1.0 / 32.0)
    inverse = 32.0 / numerators
    for n, piece in enumerate(PIECES):
        for k in range(piece[1]):
            cut = pl.ds(k * LANES, LANES)
            at = piece[0] + k
            partial = (
                keeps[n][3 * TILE : 4 * TILE, cut].astype(jnp.float32)
                + firsts[n][3 * TILE : 4 * TILE, cut].astype(jnp.float32)
            ) + (seconds[n][TILE : 2 * TILE, cut].astype(jnp.float32) + thirds[n][:, cut].astype(jnp.float32))
            coded = jnp.clip(partial * inverse[:, at : at + 1], -8.0, 8.0).astype(jnp.bfloat16)
            rows[pl.ds(at, TILE, stride=BLOCKS), :] = coded.astype(jnp.float32) * scale[:, at : at + 1]
    wide = lax.axis_index("wide")
    for j, relative in enumerate(itertools.product((1, 0), repeat=3)):
        owner = wide_near(wide, relative)
        own = pl.multiple_of(owner * BLOCKS, 8)
        other = pl.multiple_of((owner ^ 1) * BLOCKS, 8)
        send_ref[j] = rows[pl.ds(other, BLOCKS), :].astype(jnp.bfloat16)
        keep_ref[j] = rows[pl.ds(own, BLOCKS), :]


def finish(requant, keeps, firsts, seconds, thirds):
    vmem = pl.BlockSpec(memory_space=pltpu.VMEM)
    return pl.pallas_call(
        finish_kernel,
        out_shape=[
            jax.ShapeDtypeStruct((8, BLOCKS, LANES), jnp.bfloat16),
            jax.ShapeDtypeStruct((8, BLOCKS, LANES), jnp.float32),
        ],
        in_specs=[vmem] * (1 + 4 * len(PIECES)),
        out_specs=[vmem, vmem],
        scratch_shapes=[pltpu.VMEM((TILE * BLOCKS, LANES), jnp.float32)],
        compiler_params=pltpu.CompilerParams(vmem_limit_bytes=VMEM_LIMIT),
        name="finish",
    )(requant, *keeps, *firsts, *seconds, *thirds)


def adamw(gradient, params, first_moment, second_moment, step_count):
    steps = step_count[0].astype(jnp.float32)
    first = decay_first * first_moment + (1.0 - decay_first) * gradient
    second = decay_second * second_moment + (1.0 - decay_second) * gradient * gradient
    bias_first = 1.0 - jnp.power(jnp.float32(decay_first), steps)
    bias_second = 1.0 - jnp.power(jnp.float32(decay_second), steps)
    update = first / bias_first / (jnp.sqrt(second / bias_second) + epsilon) + weight_decay * params
    return (update, first, second)


def shards(grad_codes, code_scales, requant_scales, params, first_moment, second_moment, step_count):
    firsts, seconds, thirds = [], [], []
    codes = pltpu.with_memory_space_constraint(grad_codes, pltpu.HBM)
    scales = pltpu.with_memory_space_constraint(code_scales.T, pltpu.HBM)
    for piece in PIECES:
        (send,) = dequantize([(piece, 1)], codes, scales)
        firsts.append(lax.ppermute(send, AXES, pairs(piece[2][0], piece[3][0])))
    keeps = dequantize([(piece, 0) for piece in PIECES], codes, scales)
    for n, piece in enumerate(PIECES):
        send = firsts[n][: 2 * TILE].astype(jnp.float32) + keeps[n][: 2 * TILE].astype(jnp.float32)
        seconds.append(lax.ppermute(send.astype(jnp.bfloat16), AXES, pairs(piece[2][1], piece[3][1])))
    for n, piece in enumerate(PIECES):
        send = (
            firsts[n][2 * TILE : 3 * TILE].astype(jnp.float32)
            + keeps[n][2 * TILE : 3 * TILE].astype(jnp.float32)
            + seconds[n][:TILE].astype(jnp.float32)
        )
        thirds.append(lax.ppermute(send.astype(jnp.bfloat16), AXES, pairs(piece[2][2], piece[3][2])))
    send, keep = finish(requant_scales.reshape(TILE, BLOCKS), keeps, firsts, seconds, thirds)
    from_core = lax.ppermute(send, "wide", [(b, b ^ 1) for b in range(16)]).astype(jnp.float32)
    near = keep + from_core
    hops = []
    for step, count in enumerate((4, 2, 1)):
        relative = tuple(int(step == n) for n in range(3))
        route = [(b, wide_near(b, relative)) for b in range(16)]
        hops.append(lax.ppermute(near[:count].astype(jnp.bfloat16), "wide", route).astype(jnp.float32))
        near = near[count:] + hops[-1]
    tall = (BLOCKS, LANES)
    outs = adamw(
        near[0], params.reshape(tall), first_moment.reshape(tall), second_moment.reshape(tall), step_count
    )
    return tuple(out.reshape(1, COLUMNS) for out in outs)


def solution(mesh):
    in_specs = (
        P(("node", "wide"), None),
        P(("node", "wide"), None),
        P("node", "wide", None, None),
        P(("node", "wide"), None),
        P(("node", "wide"), None),
        P(("node", "wide"), None),
        P(),
    )
    out_specs = (P(("node", "wide"), None), P(("node", "wide"), None), P(("node", "wide"), None))
    return jax.shard_map(shards, mesh=mesh, in_specs=in_specs, out_specs=out_specs, check_vma=False)
```

```python
import itertools

import jax
import jax.numpy as jnp
from jax import lax
from jax.experimental import pallas as pl
from jax.experimental.pallas import tpu as pltpu
from jax.sharding import PartitionSpec as P

decay_first = 0.9
decay_second = 0.95
epsilon = 1e-08
weight_decay = 0.1

BLOCKS = 96
LANES = 128
COLUMNS = BLOCKS * LANES
TILE = 16
PIECES = (
    (0, 34, "PQZ", "PQZ", False),
    (34, 32, "QZP", "QZP", False),
    (66, 30, "ZPQ", "ZPQ", False),
)
FIRST = 0
AXES = ("node", "wide")
VMEM_LIMIT = 32 * 1024 * 1024


def bits(node):
    high = node >> 2
    return {"P": ((node >> 1) & 1) ^ high, "Q": high, "Z": node & 1}


def node_of(label):
    return (label["Q"] << 2) | ((label["P"] ^ label["Q"]) << 1) | label["Z"]


Y_FLIPS = ((3, 0), (2, 1))


def wide_at(wide, z_flip, y_flip, core):
    high = ((wide >> 2) & 1) ^ (y_flip >> 1)
    low = (((wide >> 1) ^ (wide >> 2)) & 1) ^ (y_flip & 1)
    return ((wide >> 3) ^ z_flip) << 3 | high << 2 | (high ^ low) << 1 | core


def y_route(slot):
    return [(b, wide_at(b, 0, Y_FLIPS[b & 1][slot], b & 1)) for b in range(16) if Y_FLIPS[b & 1][slot]]


def pairs(piece, *steps):
    result = []
    for node in range(8):
        for wide in range(16):
            label = bits(node)
            for step in steps:
                label[piece[2 + (wide & 1)][step]] ^= 1
            result.append((node * 16 + wide, node_of(label) * 16 + wide))
    return result


def block_row(piece, relative):
    mine = bits(lax.axis_index("node"))
    core = lax.axis_index("wide") & 1
    label = {}
    for dim in "PQZ":
        flip0 = relative[piece[2].index(dim)]
        flip1 = relative[piece[3].index(dim)]
        label[dim] = mine[dim] ^ (flip0 + core * (flip1 - flip0))
    return pl.multiple_of(node_of(label) * TILE, TILE)


ORDER = ((1, 1), (1, 0), (0, 1), (0, 0))


def dequantize_rows(piece, row, scale, codes, out):
    for k in range(piece[1]):
        at = piece[0] + k
        values = (codes(k).astype(jnp.float32) + 0.5) * scale[:, at : at + 1]
        out[:, k * LANES : (k + 1) * LANES] = values.astype(jnp.bfloat16)


def first_kernel(piece, codes_ref, scales_ref, out_ref, scales, stage, scales_buf, sem, scale_sem):
    scale_copy = pltpu.make_async_copy(scales_ref, scales_buf, scale_sem)
    scale_copy.start()
    copies = []
    for j, tail in enumerate(ORDER):
        row = block_row(piece, (1,) + tail)
        copy = pltpu.make_async_copy(
            codes_ref.at[pl.ds(row, TILE), pl.ds(piece[0] * LANES, piece[1] * LANES)],
            stage.at[pl.ds(j * TILE, TILE), :],
            sem.at[j],
        )
        copy.start()
        copies.append((row, copy))
    scale_copy.wait()
    scales[:, :BLOCKS] = scales_buf[...].T
    for j, (row, copy) in enumerate(copies):
        copy.wait()
        rows = slice(j * TILE, (j + 1) * TILE)
        dequantize_rows(
            piece,
            row,
            scales[pl.ds(row, TILE), :],
            lambda k: stage[rows, k * LANES : (k + 1) * LANES],
            out_ref.at[rows],
        )


def first_rows(piece, codes, scales_t):
    hbm = pl.BlockSpec(memory_space=pltpu.HBM)
    vmem = pl.BlockSpec(memory_space=pltpu.VMEM)
    shape = (4 * TILE, piece[1] * LANES)
    return pl.pallas_call(
        lambda *refs: first_kernel(piece, *refs),
        out_shape=jax.ShapeDtypeStruct(shape, jnp.bfloat16),
        in_specs=[hbm, hbm],
        out_specs=vmem,
        scratch_shapes=[
            pltpu.VMEM((128, LANES), jnp.float32),
            pltpu.VMEM(shape, jnp.int32),
            pltpu.VMEM((BLOCKS, 128), jnp.float32),
            pltpu.SemaphoreType.DMA((4,)),
            pltpu.SemaphoreType.DMA,
        ],
        compiler_params=pltpu.CompilerParams(vmem_limit_bytes=VMEM_LIMIT),
        name="first_rows",
    )(codes, scales_t)


def dequantize_kernel(parts, codes_ref, scales_ref, *rest):
    *outs, scales = rest
    scales[:, :BLOCKS] = scales_ref[...].T
    for (piece, first), out in zip(parts, outs):
        for j, tail in enumerate(ORDER):
            row = block_row(piece, (first,) + tail)
            dequantize_rows(
                piece,
                row,
                scales[pl.ds(row, TILE), :],
                lambda k: codes_ref[pl.ds(row, TILE), pl.ds((piece[0] + k) * LANES, LANES)],
                out.at[j * TILE : (j + 1) * TILE],
            )


def dequantize(parts, codes, scales):
    vmem = pl.BlockSpec(memory_space=pltpu.VMEM)
    return pl.pallas_call(
        lambda *refs: dequantize_kernel(parts, *refs),
        out_shape=[jax.ShapeDtypeStruct((4 * TILE, piece[1] * LANES), jnp.bfloat16) for piece, _ in parts],
        in_specs=[vmem, vmem],
        out_specs=[vmem for _ in parts],
        scratch_shapes=[pltpu.VMEM((128, LANES), jnp.float32)],
        compiler_params=pltpu.CompilerParams(vmem_limit_bytes=VMEM_LIMIT),
        name="dequantize",
    )(codes, scales)


def finish_kernel(counts, requant_ref, *refs):
    parts, (send_ref, keep_ref, rows) = refs[: sum(counts)], refs[sum(counts) :]
    numerators = requant_ref[...].astype(jnp.float32)
    scale = numerators * (1.0 / 32.0)
    inverse = 32.0 / numerators
    for n, piece in enumerate(PIECES):
        arrays = parts[sum(counts[:n]) : sum(counts[: n + 1])]
        for k in range(piece[1]):
            cut = pl.ds(k * LANES, LANES)
            at = piece[0] + k
            partial = arrays[0][arrays[0].shape[0] - TILE :, cut].astype(jnp.float32)
            for array in arrays[1:]:
                partial = partial + array[array.shape[0] - TILE :, cut].astype(jnp.float32)
            coded = jnp.clip(partial * inverse[:, at : at + 1], -8.0, 8.0).astype(jnp.bfloat16)
            rows[pl.ds(at, TILE, stride=BLOCKS), :] = coded.astype(jnp.float32) * scale[:, at : at + 1]
    wide = lax.axis_index("wide")
    core = wide & 1
    for slot in range(2):
        first, second = Y_FLIPS[0][slot], Y_FLIPS[1][slot]
        for ref, server in ((send_ref, 1 - core), (keep_ref, core)):
            y_flip = first + server * (second - first)
            for at, flip in enumerate((1, 0)):
                for owner in range(2):
                    row = pl.multiple_of(wide_at(wide, flip, y_flip, (server + owner + 1) & 1) * BLOCKS, 8)
                    ref[slot, at, owner] = rows[pl.ds(row, BLOCKS), :].astype(ref.dtype)


def finish(requant, parts):
    vmem = pl.BlockSpec(memory_space=pltpu.VMEM)
    shape = (2, 2, 2, BLOCKS, LANES)
    counts = [len(arrays) for arrays in parts]
    return pl.pallas_call(
        lambda *refs: finish_kernel(counts, *refs),
        out_shape=[jax.ShapeDtypeStruct(shape, jnp.bfloat16), jax.ShapeDtypeStruct(shape, jnp.float32)],
        in_specs=[vmem] * (1 + sum(counts)),
        out_specs=[vmem, vmem],
        scratch_shapes=[pltpu.VMEM((TILE * BLOCKS, LANES), jnp.float32)],
        compiler_params=pltpu.CompilerParams(vmem_limit_bytes=VMEM_LIMIT),
        name="finish",
    )(requant, *[array for arrays in parts for array in arrays])


def adamw(gradient, params, first_moment, second_moment, step_count):
    steps = step_count[0].astype(jnp.float32)
    first = decay_first * first_moment + (1.0 - decay_first) * gradient
    second = decay_second * second_moment + (1.0 - decay_second) * gradient * gradient
    bias_first = 1.0 - jnp.power(jnp.float32(decay_first), steps)
    bias_second = 1.0 - jnp.power(jnp.float32(decay_second), steps)
    update = first / bias_first / (jnp.sqrt(second / bias_second) + epsilon) + weight_decay * params
    return (update, first, second)


def send(array, axes, route):
    return lax.ppermute(array.astype(jnp.bfloat16), axes, route)


def total(*arrays):
    result = arrays[0].astype(jnp.float32)
    for array in arrays[1:]:
        result = result + array.astype(jnp.float32)
    return result


def shards(grad_codes, code_scales, requant_scales, params, first_moment, second_moment, step_count):
    codes = pltpu.with_memory_space_constraint(grad_codes, pltpu.HBM)
    scales = code_scales.T
    scales_hbm = pltpu.with_memory_space_constraint(scales, pltpu.HBM)
    firsts, parts = [], []
    for n, piece in enumerate(PIECES):
        if n == FIRST:
            rows = first_rows(piece, codes, scales_hbm)
        else:
            (rows,) = dequantize([(piece, 1)], grad_codes, scales)
        firsts.append(send(rows, AXES, pairs(piece, 0)))
    keeps = dequantize([(piece, 0) for piece in PIECES], grad_codes, scales)
    last = None
    for piece, first, keep in zip(PIECES, firsts, keeps):
        if last is not None:
            first, last = lax.optimization_barrier((first, last))
        parts.append([keep, first])
        if piece[4]:
            for n, steps in enumerate(((1, 2), (1,), (2,))):
                cut = slice(n * TILE, (n + 1) * TILE)
                last = total(keep[cut], first[cut]).astype(jnp.bfloat16)
                parts[-1].append(send(last, AXES, pairs(piece, *steps)))
        else:
            cut = slice(0, 2 * TILE)
            last = total(keep[cut], first[cut]).astype(jnp.bfloat16)
            parts[-1].append(send(last, AXES, pairs(piece, 1)))
    for piece, arrays in zip(PIECES, parts):
        if not piece[4]:
            arrays[2], last = lax.optimization_barrier((arrays[2], last))
            keep, first, second = arrays
            cut = slice(2 * TILE, 3 * TILE)
            last = total(keep[cut], first[cut], second[:TILE]).astype(jnp.bfloat16)
            arrays.append(send(last, AXES, pairs(piece, 2)))
    other_core = [(b, b ^ 1) for b in range(16)]
    away, near = finish(requant_scales.reshape(TILE, BLOCKS), parts)
    near = total(near, send(away, "wide", other_core))
    flipped = [send(near[slot], "wide", y_route(slot)) for slot in range(2)]
    stays = jnp.where((lax.axis_index("wide") & 1) == 0, near[1], 0.0)
    chip = total(stays, *flipped)
    chip = total(chip[1], send(chip[0], "wide", [(b, b ^ 8) for b in range(16)]))
    gradient = total(chip[1], lax.ppermute(chip[0], "wide", other_core))
    tall = (BLOCKS, LANES)
    outs = adamw(gradient, params.reshape(tall), first_moment.reshape(tall), second_moment.reshape(tall), step_count)
    return tuple(out.reshape(1, COLUMNS) for out in outs)


def solution(mesh):
    in_specs = (
        P(("node", "wide"), None),
        P(("node", "wide"), None),
        P("node", "wide", None, None),
        P(("node", "wide"), None),
        P(("node", "wide"), None),
        P(("node", "wide"), None),
        P(),
    )
    out_specs = (P(("node", "wide"), None), P(("node", "wide"), None), P(("node", "wide"), None))
    return jax.shard_map(shards, mesh=mesh, in_specs=in_specs, out_specs=out_specs, check_vma=False)
```

```python
import itertools

import jax
import jax.numpy as jnp
from jax import lax
from jax.experimental import pallas as pl
from jax.experimental.pallas import tpu as pltpu
from jax.sharding import PartitionSpec as P

decay_first = 0.9
decay_second = 0.95
epsilon = 1e-08
weight_decay = 0.1

BLOCKS = 96
LANES = 128
COLUMNS = BLOCKS * LANES
TILE = 16
PIECES = (
    (0, 34, "PZQ"),
    (34, 32, "ZQP"),
    (66, 30, "QPZ"),
)
SUMS = ((0, 1), (1, 1), (2, 1), (0, 2), (1, 2), (2, 2))
FIRST = 0
AXES = ("node", "wide")
VMEM_LIMIT = 32 * 1024 * 1024


def bits(node):
    high = node >> 2
    return {"P": ((node >> 1) & 1) ^ high, "Q": high, "Z": node & 1}


def node_of(label):
    return (label["Q"] << 2) | ((label["P"] ^ label["Q"]) << 1) | label["Z"]


Y_FLIPS = (3, 1, 2, 0)


def wide_at(wide, z_flip, y_flip, core):
    high = ((wide >> 2) & 1) ^ (y_flip >> 1)
    low = (((wide >> 1) ^ (wide >> 2)) & 1) ^ (y_flip & 1)
    return ((wide >> 3) ^ z_flip) << 3 | high << 2 | (high ^ low) << 1 | core


def pairs(piece, *steps):
    result = []
    for node in range(8):
        for wide in range(16):
            label = bits(node)
            for step in steps:
                label[piece[2][step]] ^= 1
            result.append((node * 16 + wide, node_of(label) * 16 + wide))
    return result


def block_row(piece, relative):
    mine = bits(lax.axis_index("node"))
    label = {dim: mine[dim] ^ relative[piece[2].index(dim)] for dim in "PQZ"}
    return pl.multiple_of(node_of(label) * TILE, TILE)


ORDER = ((1, 1), (1, 0), (0, 1), (0, 0))


def dequantize_rows(piece, row, scale, codes, out):
    for k in range(piece[1]):
        at = piece[0] + k
        values = (codes(k).astype(jnp.float32) + 0.5) * scale[:, at : at + 1]
        out[:, k * LANES : (k + 1) * LANES] = values.astype(jnp.bfloat16)


def first_kernel(piece, codes_ref, scales_ref, out_ref, scales, stage, scales_buf, sem, scale_sem):
    scale_copy = pltpu.make_async_copy(scales_ref, scales_buf, scale_sem)
    scale_copy.start()
    copies = []
    for j, tail in enumerate(ORDER):
        row = block_row(piece, (1,) + tail)
        copy = pltpu.make_async_copy(
            codes_ref.at[pl.ds(row, TILE), pl.ds(piece[0] * LANES, piece[1] * LANES)],
            stage.at[pl.ds(j * TILE, TILE), :],
            sem.at[j],
        )
        copy.start()
        copies.append((row, copy))
    scale_copy.wait()
    scales[:, :BLOCKS] = scales_buf[...].T
    for j, (row, copy) in enumerate(copies):
        copy.wait()
        rows = slice(j * TILE, (j + 1) * TILE)
        dequantize_rows(
            piece,
            row,
            scales[pl.ds(row, TILE), :],
            lambda k: stage[rows, k * LANES : (k + 1) * LANES],
            out_ref.at[rows],
        )


def first_rows(piece, codes, scales_t):
    hbm = pl.BlockSpec(memory_space=pltpu.HBM)
    vmem = pl.BlockSpec(memory_space=pltpu.VMEM)
    shape = (4 * TILE, piece[1] * LANES)
    return pl.pallas_call(
        lambda *refs: first_kernel(piece, *refs),
        out_shape=jax.ShapeDtypeStruct(shape, jnp.bfloat16),
        in_specs=[hbm, hbm],
        out_specs=vmem,
        scratch_shapes=[
            pltpu.VMEM((128, LANES), jnp.float32),
            pltpu.VMEM(shape, jnp.int32),
            pltpu.VMEM((BLOCKS, 128), jnp.float32),
            pltpu.SemaphoreType.DMA((4,)),
            pltpu.SemaphoreType.DMA,
        ],
        compiler_params=pltpu.CompilerParams(vmem_limit_bytes=VMEM_LIMIT),
        name="first_rows",
    )(codes, scales_t)


def dequantize_kernel(parts, codes_ref, scales_ref, *rest):
    *outs, scales = rest
    scales[:, :BLOCKS] = scales_ref[...].T
    for (piece, first), out in zip(parts, outs):
        for j, tail in enumerate(ORDER):
            row = block_row(piece, (first,) + tail)
            dequantize_rows(
                piece,
                row,
                scales[pl.ds(row, TILE), :],
                lambda k: codes_ref[pl.ds(row, TILE), pl.ds((piece[0] + k) * LANES, LANES)],
                out.at[j * TILE : (j + 1) * TILE],
            )


def dequantize(parts, codes, scales):
    vmem = pl.BlockSpec(memory_space=pltpu.VMEM)
    return pl.pallas_call(
        lambda *refs: dequantize_kernel(parts, *refs),
        out_shape=[jax.ShapeDtypeStruct((4 * TILE, piece[1] * LANES), jnp.bfloat16) for piece, _ in parts],
        in_specs=[vmem, vmem],
        out_specs=[vmem for _ in parts],
        scratch_shapes=[pltpu.VMEM((128, LANES), jnp.float32)],
        compiler_params=pltpu.CompilerParams(vmem_limit_bytes=VMEM_LIMIT),
        name="dequantize",
    )(codes, scales)


def finish_kernel(counts, requant_ref, *refs):
    parts, (send_ref, keep_ref, rows) = refs[: sum(counts)], refs[sum(counts) :]
    numerators = requant_ref[...].astype(jnp.float32)
    scale = numerators * (1.0 / 32.0)
    inverse = 32.0 / numerators
    for n, piece in enumerate(PIECES):
        arrays = parts[sum(counts[:n]) : sum(counts[: n + 1])]
        for k in range(piece[1]):
            cut = pl.ds(k * LANES, LANES)
            at = piece[0] + k
            partial = arrays[0][arrays[0].shape[0] - TILE :, cut].astype(jnp.float32)
            for array in arrays[1:]:
                partial = partial + array[array.shape[0] - TILE :, cut].astype(jnp.float32)
            coded = jnp.clip(partial * inverse[:, at : at + 1], -8.0, 8.0).astype(jnp.bfloat16)
            rows[pl.ds(at, TILE, stride=BLOCKS), :] = coded.astype(jnp.float32) * scale[:, at : at + 1]
    wide = lax.axis_index("wide")
    core = wide & 1
    for slot, y_flip in enumerate(Y_FLIPS):
        for z_slot, z_flip in enumerate((1, 0)):
            for ref, owner in ((send_ref, 1 - core), (keep_ref, core)):
                row = pl.multiple_of(wide_at(wide, z_flip, y_flip, owner) * BLOCKS, 8)
                ref[slot, z_slot] = rows[pl.ds(row, BLOCKS), :].astype(ref.dtype)


def finish(requant, parts):
    vmem = pl.BlockSpec(memory_space=pltpu.VMEM)
    shape = (4, 2, BLOCKS, LANES)
    counts = [len(arrays) for arrays in parts]
    return pl.pallas_call(
        lambda *refs: finish_kernel(counts, *refs),
        out_shape=[jax.ShapeDtypeStruct(shape, jnp.bfloat16), jax.ShapeDtypeStruct(shape, jnp.float32)],
        in_specs=[vmem] * (1 + sum(counts)),
        out_specs=[vmem, vmem],
        scratch_shapes=[pltpu.VMEM((TILE * BLOCKS, LANES), jnp.float32)],
        compiler_params=pltpu.CompilerParams(vmem_limit_bytes=VMEM_LIMIT),
        name="finish",
    )(requant, *[array for arrays in parts for array in arrays])


def adamw(gradient, params, first_moment, second_moment, step_count):
    steps = step_count[0].astype(jnp.float32)
    first = decay_first * first_moment + (1.0 - decay_first) * gradient
    second = decay_second * second_moment + (1.0 - decay_second) * gradient * gradient
    bias_first = 1.0 - jnp.power(jnp.float32(decay_first), steps)
    bias_second = 1.0 - jnp.power(jnp.float32(decay_second), steps)
    update = first / bias_first / (jnp.sqrt(second / bias_second) + epsilon) + weight_decay * params
    return (update, first, second)


def send(array, axes, route):
    return lax.ppermute(array.astype(jnp.bfloat16), axes, route)


def total(*arrays):
    result = arrays[0].astype(jnp.float32)
    for array in arrays[1:]:
        result = result + array.astype(jnp.float32)
    return result


def shards(grad_codes, code_scales, requant_scales, params, first_moment, second_moment, step_count):
    codes = pltpu.with_memory_space_constraint(grad_codes, pltpu.HBM)
    scales = code_scales.T
    scales_hbm = pltpu.with_memory_space_constraint(scales, pltpu.HBM)
    firsts = []
    for n, piece in enumerate(PIECES):
        if n == FIRST:
            rows = first_rows(piece, codes, scales_hbm)
        else:
            (rows,) = dequantize([(piece, 1)], grad_codes, scales)
        firsts.append(send(rows, AXES, pairs(piece, 0)))
    keeps = dequantize([(piece, 0) for piece in PIECES], grad_codes, scales)
    parts = [[keep, first] for keep, first in zip(keeps, firsts)]
    last = None
    for n, step in SUMS:
        if last is not None:
            parts[n][step], last = lax.optimization_barrier((parts[n][step], last))
        cut = slice(0, 2 * TILE) if step == 1 else slice(2 * TILE, 3 * TILE)
        last = total(*[array[cut] for array in parts[n][:2]], *[array[:TILE] for array in parts[n][2:]])
        last = last.astype(jnp.bfloat16)
        parts[n].append(send(last, AXES, pairs(PIECES[n], step)))
    other_core = [(b, b ^ 1) for b in range(16)]
    away, near = finish(requant_scales.reshape(TILE, BLOCKS), parts)
    near = total(near, send(away, "wide", other_core))
    routes = [[(b, wide_at(b, 0, y_flip, b & 1)) for b in range(16)] for y_flip in Y_FLIPS[:3]]
    chip = total(near[3], *[send(near[slot], "wide", route) for slot, route in enumerate(routes)])
    gradient = total(chip[1], send(chip[0], "wide", [(b, b ^ 8) for b in range(16)]))
    tall = (BLOCKS, LANES)
    outs = adamw(gradient, params.reshape(tall), first_moment.reshape(tall), second_moment.reshape(tall), step_count)
    return tuple(out.reshape(1, COLUMNS) for out in outs)


def solution(mesh):
    in_specs = (
        P(("node", "wide"), None),
        P(("node", "wide"), None),
        P("node", "wide", None, None),
        P(("node", "wide"), None),
        P(("node", "wide"), None),
        P(("node", "wide"), None),
        P(),
    )
    out_specs = (P(("node", "wide"), None), P(("node", "wide"), None), P(("node", "wide"), None))
    return jax.shard_map(shards, mesh=mesh, in_specs=in_specs, out_specs=out_specs, check_vma=False)
```

```python
import itertools

import jax
import jax.numpy as jnp
from jax import lax
from jax.experimental import pallas as pl
from jax.experimental.pallas import tpu as pltpu
from jax.sharding import PartitionSpec as P

decay_first = 0.9
decay_second = 0.95
epsilon = 1e-08
weight_decay = 0.1

BLOCKS = 96
LANES = 128
COLUMNS = BLOCKS * LANES
TILE = 16
PIECES = (
    (0, 34, "PZQ"),
    (34, 32, "ZQP"),
    (66, 30, "QPZ"),
)
SUMS = ((0, 1), (1, 1), (2, 1), (0, 2), (1, 2), (2, 2))
EARLY = 1
FIRST = 0
AXES = ("node", "wide")
VMEM_LIMIT = 32 * 1024 * 1024


def bits(node):
    high = node >> 2
    return {"P": ((node >> 1) & 1) ^ high, "Q": high, "Z": node & 1}


def node_of(label):
    return (label["Q"] << 2) | ((label["P"] ^ label["Q"]) << 1) | label["Z"]


Y_FLIPS = (3, 1, 2, 0)


def wide_at(wide, z_flip, y_flip, core):
    high = ((wide >> 2) & 1) ^ (y_flip >> 1)
    low = (((wide >> 1) ^ (wide >> 2)) & 1) ^ (y_flip & 1)
    return ((wide >> 3) ^ z_flip) << 3 | high << 2 | (high ^ low) << 1 | core


def pairs(piece, *steps):
    result = []
    for node in range(8):
        for wide in range(16):
            label = bits(node)
            for step in steps:
                label[piece[2][step]] ^= 1
            result.append((node * 16 + wide, node_of(label) * 16 + wide))
    return result


def block_row(piece, relative):
    mine = bits(lax.axis_index("node"))
    label = {dim: mine[dim] ^ relative[piece[2].index(dim)] for dim in "PQZ"}
    return pl.multiple_of(node_of(label) * TILE, TILE)


ORDER = ((1, 1), (1, 0), (0, 1), (0, 0))


def block_range(pieces):
    return pieces[0][0] // 8 * 8, pl.cdiv(pieces[-1][0] + pieces[-1][1], 8) * 8


def dequantize_rows(piece, row, scale, codes, out):
    for k in range(piece[1]):
        at = piece[0] + k - scale[1]
        values = (codes(k).astype(jnp.float32) + 0.5) * scale[0][:, at : at + 1]
        out[:, k * LANES : (k + 1) * LANES] = values.astype(jnp.bfloat16)


def first_kernel(piece, codes_ref, scales_ref, out_ref, scales, stage, scales_buf, sem, scale_sem):
    low, high = block_range([piece])
    scale_copy = pltpu.make_async_copy(scales_ref.at[low:high], scales_buf, scale_sem)
    scale_copy.start()
    copies = []
    for j, tail in enumerate(ORDER):
        row = block_row(piece, (1,) + tail)
        copy = pltpu.make_async_copy(
            codes_ref.at[pl.ds(row, TILE), pl.ds(piece[0] * LANES, piece[1] * LANES)],
            stage.at[pl.ds(j * TILE, TILE), :],
            sem.at[j],
        )
        copy.start()
        copies.append((row, copy))
    scale_copy.wait()
    scales[:, : high - low] = scales_buf[...].T
    for j, (row, copy) in enumerate(copies):
        copy.wait()
        rows = slice(j * TILE, (j + 1) * TILE)
        dequantize_rows(
            piece,
            row,
            (scales[pl.ds(row, TILE), :], low),
            lambda k: stage[rows, k * LANES : (k + 1) * LANES],
            out_ref.at[rows],
        )


def first_rows(piece, codes, scales_t):
    low, high = block_range([piece])
    hbm = pl.BlockSpec(memory_space=pltpu.HBM)
    vmem = pl.BlockSpec(memory_space=pltpu.VMEM)
    shape = (4 * TILE, piece[1] * LANES)
    return pl.pallas_call(
        lambda *refs: first_kernel(piece, *refs),
        out_shape=jax.ShapeDtypeStruct(shape, jnp.bfloat16),
        in_specs=[hbm, hbm],
        out_specs=vmem,
        scratch_shapes=[
            pltpu.VMEM((128, LANES), jnp.float32),
            pltpu.VMEM(shape, jnp.int32),
            pltpu.VMEM((high - low, 128), jnp.float32),
            pltpu.SemaphoreType.DMA((4,)),
            pltpu.SemaphoreType.DMA,
        ],
        compiler_params=pltpu.CompilerParams(vmem_limit_bytes=VMEM_LIMIT),
        name="first_rows",
    )(codes, scales_t)


def dequantize_kernel(parts, codes_ref, scales_ref, *rest):
    *outs, scales = rest
    low, high = block_range([piece for piece, _ in parts])
    scales[:, : high - low] = scales_ref[low:high].T
    for (piece, first), out in zip(parts, outs):
        for j, tail in enumerate(ORDER):
            row = block_row(piece, (first,) + tail)
            dequantize_rows(
                piece,
                row,
                (scales[pl.ds(row, TILE), :], low),
                lambda k: codes_ref[pl.ds(row, TILE), pl.ds((piece[0] + k) * LANES, LANES)],
                out.at[j * TILE : (j + 1) * TILE],
            )


def dequantize(parts, codes, scales):
    vmem = pl.BlockSpec(memory_space=pltpu.VMEM)
    return pl.pallas_call(
        lambda *refs: dequantize_kernel(parts, *refs),
        out_shape=[jax.ShapeDtypeStruct((4 * TILE, piece[1] * LANES), jnp.bfloat16) for piece, _ in parts],
        in_specs=[vmem, vmem],
        out_specs=[vmem for _ in parts],
        scratch_shapes=[pltpu.VMEM((128, LANES), jnp.float32)],
        compiler_params=pltpu.CompilerParams(vmem_limit_bytes=VMEM_LIMIT),
        name="dequantize",
    )(codes, scales)


def finish_kernel(pieces, counts, requant_ref, *refs):
    parts, (send_ref, keep_ref, rows) = refs[: sum(counts)], refs[-3:]
    numerators = requant_ref[...].astype(jnp.float32)
    scale = numerators * (1.0 / 32.0)
    inverse = 32.0 / numerators
    start, blocks = pieces[0][0], sum(piece[1] for piece in pieces)
    stride = rows.shape[0] // TILE
    for n, piece in enumerate(pieces):
        arrays = parts[sum(counts[:n]) : sum(counts[: n + 1])]
        for k in range(piece[1]):
            cut = pl.ds(k * LANES, LANES)
            at = piece[0] + k
            partial = arrays[0][arrays[0].shape[0] - TILE :, cut].astype(jnp.float32)
            for array in arrays[1:]:
                partial = partial + array[array.shape[0] - TILE :, cut].astype(jnp.float32)
            coded = jnp.clip(partial * inverse[:, at : at + 1], -8.0, 8.0).astype(jnp.bfloat16)
            rows[pl.ds(at - start, TILE, stride=stride), :] = coded.astype(jnp.float32) * scale[:, at : at + 1]
    wide = lax.axis_index("wide")
    core = wide & 1
    for slot, y_flip in enumerate(Y_FLIPS):
        for z_slot, z_flip in enumerate((1, 0)):
            for ref, owner in ((send_ref, 1 - core), (keep_ref, core)):
                row = pl.multiple_of(wide_at(wide, z_flip, y_flip, owner) * stride, 8)
                ref[slot, z_slot] = rows[pl.ds(row, blocks), :].astype(ref.dtype)


def finish(requant, pieces, parts):
    vmem = pl.BlockSpec(memory_space=pltpu.VMEM)
    blocks = sum(piece[1] for piece in pieces)
    shape = (4, 2, blocks, LANES)
    counts = [len(arrays) for arrays in parts]
    inputs = [requant, *[array for arrays in parts for array in arrays]]
    return pl.pallas_call(
        lambda *refs: finish_kernel(pieces, counts, *refs),
        out_shape=[jax.ShapeDtypeStruct(shape, jnp.bfloat16), jax.ShapeDtypeStruct(shape, jnp.float32)],
        in_specs=[vmem] * len(inputs),
        out_specs=[vmem, vmem],
        scratch_shapes=[pltpu.VMEM((TILE * pl.cdiv(blocks, 8) * 8, LANES), jnp.float32)],
        compiler_params=pltpu.CompilerParams(vmem_limit_bytes=VMEM_LIMIT),
        name="finish",
    )(*inputs)


def adamw(gradient, params, first_moment, second_moment, step_count):
    steps = step_count[0].astype(jnp.float32)
    first = decay_first * first_moment + (1.0 - decay_first) * gradient
    second = decay_second * second_moment + (1.0 - decay_second) * gradient * gradient
    bias_first = 1.0 - jnp.power(jnp.float32(decay_first), steps)
    bias_second = 1.0 - jnp.power(jnp.float32(decay_second), steps)
    update = first / bias_first / (jnp.sqrt(second / bias_second) + epsilon) + weight_decay * params
    return (update, first, second)


def send(array, axes, route):
    return lax.ppermute(array.astype(jnp.bfloat16), axes, route)


def total(*arrays):
    result = arrays[0].astype(jnp.float32)
    for array in arrays[1:]:
        result = result + array.astype(jnp.float32)
    return result


def shards(grad_codes, code_scales, requant_scales, params, first_moment, second_moment, step_count):
    codes = pltpu.with_memory_space_constraint(grad_codes, pltpu.HBM)
    scales = code_scales.T
    scales_hbm = pltpu.with_memory_space_constraint(scales, pltpu.HBM)
    firsts = []
    for n, piece in enumerate(PIECES):
        if n == FIRST:
            rows = first_rows(piece, codes, scales_hbm)
        else:
            (rows,) = dequantize([(piece, 1)], grad_codes, scales)
        firsts.append(send(rows, AXES, pairs(piece, 0)))
    keeps = dequantize([(piece, 0) for piece in PIECES], grad_codes, scales)
    parts = [[keep, first] for keep, first in zip(keeps, firsts)]
    last = None
    for n, step in SUMS:
        if last is not None:
            parts[n][step], last = lax.optimization_barrier((parts[n][step], last))
        cut = slice(0, 2 * TILE) if step == 1 else slice(2 * TILE, 3 * TILE)
        last = total(*[array[cut] for array in parts[n][:2]], *[array[:TILE] for array in parts[n][2:]])
        last = last.astype(jnp.bfloat16)
        parts[n].append(send(last, AXES, pairs(PIECES[n], step)))
    other_core = [(b, b ^ 1) for b in range(16)]
    requant = requant_scales.reshape(TILE, BLOCKS)
    near = []
    for cut in (slice(0, EARLY), slice(EARLY, None)):
        away, keep = finish(requant, PIECES[cut], parts[cut])
        requant, away = lax.optimization_barrier((requant, away))
        near.append(total(keep, send(away, "wide", [(b, b ^ 1) for b in range(16)])))
    near = jnp.concatenate(near, axis=2)
    routes = [[(b, wide_at(b, 0, y_flip, b & 1)) for b in range(16)] for y_flip in Y_FLIPS[:3]]
    chip = total(near[3], *[send(near[slot], "wide", route) for slot, route in enumerate(routes)])
    gradient = total(chip[1], send(chip[0], "wide", [(b, b ^ 8) for b in range(16)]))
    tall = (BLOCKS, LANES)
    outs = adamw(gradient, params.reshape(tall), first_moment.reshape(tall), second_moment.reshape(tall), step_count)
    return tuple(out.reshape(1, COLUMNS) for out in outs)


def solution(mesh):
    in_specs = (
        P(("node", "wide"), None),
        P(("node", "wide"), None),
        P("node", "wide", None, None),
        P(("node", "wide"), None),
        P(("node", "wide"), None),
        P(("node", "wide"), None),
        P(),
    )
    out_specs = (P(("node", "wide"), None), P(("node", "wide"), None), P(("node", "wide"), None))
    return jax.shard_map(shards, mesh=mesh, in_specs=in_specs, out_specs=out_specs, check_vma=False)
```

```python
import itertools

import jax
import jax.numpy as jnp
from jax import lax
from jax.experimental import pallas as pl
from jax.experimental.pallas import tpu as pltpu
from jax.sharding import PartitionSpec as P

decay_first = 0.9
decay_second = 0.95
epsilon = 1e-08
weight_decay = 0.1

BLOCKS = 96
LANES = 128
COLUMNS = BLOCKS * LANES
TILE = 16
PIECES = (
    (0, 34, "PZQ"),
    (34, 32, "ZQP"),
    (66, 30, "QPZ"),
)
SUMS = ((0, 1), (1, 1), (2, 1), (0, 2), (1, 2), (2, 2))
EARLY = 1
FIRST = 0
AXES = ("node", "wide")
VMEM_LIMIT = 32 * 1024 * 1024


def bits(node):
    high = node >> 2
    return {"P": ((node >> 1) & 1) ^ high, "Q": high, "Z": node & 1}


def node_of(label):
    return (label["Q"] << 2) | ((label["P"] ^ label["Q"]) << 1) | label["Z"]


Y_FLIPS = (3, 1, 2, 0)


def wide_at(wide, z_flip, y_flip, core):
    high = ((wide >> 2) & 1) ^ (y_flip >> 1)
    low = (((wide >> 1) ^ (wide >> 2)) & 1) ^ (y_flip & 1)
    return ((wide >> 3) ^ z_flip) << 3 | high << 2 | (high ^ low) << 1 | core


def pairs(piece, *steps):
    result = []
    for node in range(8):
        for wide in range(16):
            label = bits(node)
            for step in steps:
                label[piece[2][step]] ^= 1
            result.append((node * 16 + wide, node_of(label) * 16 + wide))
    return result


def block_row(piece, relative):
    mine = bits(lax.axis_index("node"))
    label = {dim: mine[dim] ^ relative[piece[2].index(dim)] for dim in "PQZ"}
    return pl.multiple_of(node_of(label) * TILE, TILE)


ORDER = ((1, 1), (1, 0), (0, 1), (0, 0))


def block_range(pieces):
    return pieces[0][0] // 8 * 8, pl.cdiv(pieces[-1][0] + pieces[-1][1], 8) * 8


def dequantize_rows(piece, row, scale, codes, out):
    for k in range(piece[1]):
        at = piece[0] + k - scale[1]
        values = (codes(k).astype(jnp.float32) + 0.5) * scale[0][:, at : at + 1]
        out[:, k * LANES : (k + 1) * LANES] = values.astype(jnp.bfloat16)


def first_kernel(piece, codes_ref, scales_ref, out_ref, scales, stage, scales_buf, sem, scale_sem):
    low, high = block_range([piece])
    scale_copy = pltpu.make_async_copy(scales_ref.at[low:high], scales_buf, scale_sem)
    scale_copy.start()
    copies = []
    for j, tail in enumerate(ORDER):
        row = block_row(piece, (1,) + tail)
        copy = pltpu.make_async_copy(
            codes_ref.at[pl.ds(row, TILE), pl.ds(piece[0] * LANES, piece[1] * LANES)],
            stage.at[pl.ds(j * TILE, TILE), :],
            sem.at[j],
        )
        copy.start()
        copies.append((row, copy))
    scale_copy.wait()
    scales[:, : high - low] = scales_buf[...].T
    for j, (row, copy) in enumerate(copies):
        copy.wait()
        rows = slice(j * TILE, (j + 1) * TILE)
        dequantize_rows(
            piece,
            row,
            (scales[pl.ds(row, TILE), :], low),
            lambda k: stage[rows, k * LANES : (k + 1) * LANES],
            out_ref.at[rows],
        )


def first_rows(piece, codes, scales_t):
    low, high = block_range([piece])
    hbm = pl.BlockSpec(memory_space=pltpu.HBM)
    vmem = pl.BlockSpec(memory_space=pltpu.VMEM)
    shape = (4 * TILE, piece[1] * LANES)
    return pl.pallas_call(
        lambda *refs: first_kernel(piece, *refs),
        out_shape=jax.ShapeDtypeStruct(shape, jnp.bfloat16),
        in_specs=[hbm, hbm],
        out_specs=vmem,
        scratch_shapes=[
            pltpu.VMEM((128, LANES), jnp.float32),
            pltpu.VMEM(shape, jnp.int32),
            pltpu.VMEM((high - low, 128), jnp.float32),
            pltpu.SemaphoreType.DMA((4,)),
            pltpu.SemaphoreType.DMA,
        ],
        compiler_params=pltpu.CompilerParams(vmem_limit_bytes=VMEM_LIMIT),
        name="first_rows",
    )(codes, scales_t)


def dequantize_kernel(parts, codes_ref, scales_ref, *rest):
    *outs, scales = rest
    low, high = block_range([piece for piece, _ in parts])
    scales[:, : high - low] = scales_ref[low:high].T
    for (piece, first), out in zip(parts, outs):
        for j, tail in enumerate(ORDER):
            row = block_row(piece, (first,) + tail)
            dequantize_rows(
                piece,
                row,
                (scales[pl.ds(row, TILE), :], low),
                lambda k: codes_ref[pl.ds(row, TILE), pl.ds((piece[0] + k) * LANES, LANES)],
                out.at[j * TILE : (j + 1) * TILE],
            )


def dequantize(parts, codes, scales):
    vmem = pl.BlockSpec(memory_space=pltpu.VMEM)
    return pl.pallas_call(
        lambda *refs: dequantize_kernel(parts, *refs),
        out_shape=[jax.ShapeDtypeStruct((4 * TILE, piece[1] * LANES), jnp.bfloat16) for piece, _ in parts],
        in_specs=[vmem, vmem],
        out_specs=[vmem for _ in parts],
        scratch_shapes=[pltpu.VMEM((128, LANES), jnp.float32)],
        compiler_params=pltpu.CompilerParams(vmem_limit_bytes=VMEM_LIMIT),
        name="dequantize",
    )(codes, scales)


def finish_kernel(pieces, counts, requant_ref, *refs):
    parts, (send_ref, keep_ref, rows) = refs[: sum(counts)], refs[-3:]
    numerators = requant_ref[...].astype(jnp.float32)
    scale = numerators * (1.0 / 32.0)
    inverse = 32.0 / numerators
    start, blocks = pieces[0][0], sum(piece[1] for piece in pieces)
    stride = rows.shape[0] // (TILE + 1)
    for n, piece in enumerate(pieces):
        arrays = parts[sum(counts[:n]) : sum(counts[: n + 1])]
        for k in range(piece[1]):
            cut = pl.ds(k * LANES, LANES)
            at = piece[0] + k
            partial = arrays[0][arrays[0].shape[0] - TILE :, cut].astype(jnp.float32)
            for array in arrays[1:]:
                partial = partial + array[array.shape[0] - TILE :, cut].astype(jnp.float32)
            coded = jnp.clip(partial * inverse[:, at : at + 1], -8.0, 8.0).astype(jnp.bfloat16)
            rows[pl.ds(at - start, TILE, stride=stride), :] = coded.astype(jnp.float32) * scale[:, at : at + 1]
    wide = lax.axis_index("wide")
    core = wide & 1
    for slot, y_flip in enumerate(Y_FLIPS):
        for z_slot, z_flip in enumerate((1, 0)):
            for ref, owner in ((send_ref, 1 - core), (keep_ref, core)):
                row = pl.multiple_of(wide_at(wide, z_flip, y_flip, owner) * stride, 8)
                ref[slot, z_slot] = rows[pl.ds(row, blocks), :].astype(ref.dtype)


def finish(requant, pieces, parts):
    vmem = pl.BlockSpec(memory_space=pltpu.VMEM)
    blocks = sum(piece[1] for piece in pieces)
    shape = (4, 2, blocks, LANES)
    counts = [len(arrays) for arrays in parts]
    inputs = [requant, *[array for arrays in parts for array in arrays]]
    return pl.pallas_call(
        lambda *refs: finish_kernel(pieces, counts, *refs),
        out_shape=[jax.ShapeDtypeStruct(shape, jnp.bfloat16), jax.ShapeDtypeStruct(shape, jnp.float32)],
        in_specs=[vmem] * len(inputs),
        out_specs=[vmem, vmem],
        scratch_shapes=[pltpu.VMEM(((TILE + 1) * pl.cdiv(blocks, 8) * 8, LANES), jnp.float32)],
        compiler_params=pltpu.CompilerParams(vmem_limit_bytes=VMEM_LIMIT),
        name="finish",
    )(*inputs)


def adamw(gradient, params, first_moment, second_moment, step_count):
    steps = step_count[0].astype(jnp.float32)
    first = decay_first * first_moment + (1.0 - decay_first) * gradient
    second = decay_second * second_moment + (1.0 - decay_second) * gradient * gradient
    bias_first = 1.0 - jnp.power(jnp.float32(decay_first), steps)
    bias_second = 1.0 - jnp.power(jnp.float32(decay_second), steps)
    update = first / bias_first / (jnp.sqrt(second / bias_second) + epsilon) + weight_decay * params
    return (update, first, second)


def send(array, axes, route):
    return lax.ppermute(array.astype(jnp.bfloat16), axes, route)


def total(*arrays):
    result = arrays[0].astype(jnp.float32)
    for array in arrays[1:]:
        result = result + array.astype(jnp.float32)
    return result


def shards(grad_codes, code_scales, requant_scales, params, first_moment, second_moment, step_count):
    codes = pltpu.with_memory_space_constraint(grad_codes, pltpu.HBM)
    scales = code_scales.T
    scales_hbm = pltpu.with_memory_space_constraint(scales, pltpu.HBM)
    firsts = []
    for n, piece in enumerate(PIECES):
        if n == FIRST:
            rows = first_rows(piece, codes, scales_hbm)
        else:
            (rows,) = dequantize([(piece, 1)], grad_codes, scales)
        firsts.append(send(rows, AXES, pairs(piece, 0)))
    keeps = dequantize([(piece, 0) for piece in PIECES], grad_codes, scales)
    parts = [[keep, first] for keep, first in zip(keeps, firsts)]
    last = None
    for n, step in SUMS:
        if last is not None:
            parts[n][step], last = lax.optimization_barrier((parts[n][step], last))
        cut = slice(0, 2 * TILE) if step == 1 else slice(2 * TILE, 3 * TILE)
        last = total(*[array[cut] for array in parts[n][:2]], *[array[:TILE] for array in parts[n][2:]])
        last = last.astype(jnp.bfloat16)
        parts[n].append(send(last, AXES, pairs(PIECES[n], step)))
    other_core = [(b, b ^ 1) for b in range(16)]
    requant = requant_scales.reshape(TILE, BLOCKS)
    near = []
    for cut in (slice(0, EARLY), slice(EARLY, None)):
        away, keep = finish(requant, PIECES[cut], parts[cut])
        requant, away = lax.optimization_barrier((requant, away))
        near.append(total(keep, send(away, "wide", [(b, b ^ 1) for b in range(16)])))
    near = jnp.concatenate(near, axis=2)
    routes = [[(b, wide_at(b, 0, y_flip, b & 1)) for b in range(16)] for y_flip in Y_FLIPS[:3]]
    chip = total(near[3], *[send(near[slot], "wide", route) for slot, route in enumerate(routes)])
    gradient = total(chip[1], send(chip[0], "wide", [(b, b ^ 8) for b in range(16)]))
    tall = (BLOCKS, LANES)
    outs = adamw(gradient, params.reshape(tall), first_moment.reshape(tall), second_moment.reshape(tall), step_count)
    return tuple(out.reshape(1, COLUMNS) for out in outs)


def solution(mesh):
    in_specs = (
        P(("node", "wide"), None),
        P(("node", "wide"), None),
        P("node", "wide", None, None),
        P(("node", "wide"), None),
        P(("node", "wide"), None),
        P(("node", "wide"), None),
        P(),
    )
    out_specs = (P(("node", "wide"), None), P(("node", "wide"), None), P(("node", "wide"), None))
    return jax.shard_map(shards, mesh=mesh, in_specs=in_specs, out_specs=out_specs, check_vma=False)
```

```python
import itertools

import jax
import jax.numpy as jnp
from jax import lax
from jax.experimental import pallas as pl
from jax.experimental.pallas import tpu as pltpu
from jax.sharding import PartitionSpec as P

decay_first = 0.9
decay_second = 0.95
epsilon = 1e-08
weight_decay = 0.1

BLOCKS = 96
LANES = 128
COLUMNS = BLOCKS * LANES
TILE = 16
PIECES = (
    (0, 32, "PZQ"),
    (32, 33, "ZQP"),
    (65, 31, "QPZ"),
)
SUMS = ((0, 1), (1, 1), (2, 1), (0, 2), (1, 2), (2, 2))
EARLY = 1
FIRST = 0
AXES = ("node", "wide")
VMEM_LIMIT = 32 * 1024 * 1024


def bits(node):
    high = node >> 2
    return {"P": ((node >> 1) & 1) ^ high, "Q": high, "Z": node & 1}


def node_of(label):
    return (label["Q"] << 2) | ((label["P"] ^ label["Q"]) << 1) | label["Z"]


Y_FLIPS = (3, 1, 2, 0)


def wide_at(wide, z_flip, y_flip, core):
    high = ((wide >> 2) & 1) ^ (y_flip >> 1)
    low = (((wide >> 1) ^ (wide >> 2)) & 1) ^ (y_flip & 1)
    return ((wide >> 3) ^ z_flip) << 3 | high << 2 | (high ^ low) << 1 | core


def pairs(piece, *steps):
    result = []
    for node in range(8):
        for wide in range(16):
            label = bits(node)
            for step in steps:
                label[piece[2][step]] ^= 1
            result.append((node * 16 + wide, node_of(label) * 16 + wide))
    return result


def block_row(piece, relative):
    mine = bits(lax.axis_index("node"))
    label = {dim: mine[dim] ^ relative[piece[2].index(dim)] for dim in "PQZ"}
    return pl.multiple_of(node_of(label) * TILE, TILE)


ORDER = ((1, 1), (1, 0), (0, 1), (0, 0))


def block_range(pieces):
    return pieces[0][0] // 8 * 8, pl.cdiv(pieces[-1][0] + pieces[-1][1], 8) * 8


def dequantize_rows(piece, row, scale, codes, out):
    for k in range(piece[1]):
        at = piece[0] + k - scale[1]
        values = (codes(k).astype(jnp.float32) + 0.5) * scale[0][:, at : at + 1]
        out[:, k * LANES : (k + 1) * LANES] = values.astype(jnp.bfloat16)


def first_kernel(piece, codes_ref, scales_ref, out_ref, scales, stage, scales_buf, sem, scale_sem):
    low, high = block_range([piece])
    scale_copy = pltpu.make_async_copy(scales_ref.at[low:high], scales_buf, scale_sem)
    scale_copy.start()
    copies = []
    for j, tail in enumerate(ORDER):
        row = block_row(piece, (1,) + tail)
        copy = pltpu.make_async_copy(
            codes_ref.at[pl.ds(row, TILE), pl.ds(piece[0] * LANES, piece[1] * LANES)],
            stage.at[pl.ds(j * TILE, TILE), :],
            sem.at[j],
        )
        copy.start()
        copies.append((row, copy))
    scale_copy.wait()
    scales[:, : high - low] = scales_buf[...].T
    for j, (row, copy) in enumerate(copies):
        copy.wait()
        rows = slice(j * TILE, (j + 1) * TILE)
        dequantize_rows(
            piece,
            row,
            (scales[pl.ds(row, TILE), :], low),
            lambda k: stage[rows, k * LANES : (k + 1) * LANES],
            out_ref.at[rows],
        )


def first_rows(piece, codes, scales_t):
    low, high = block_range([piece])
    hbm = pl.BlockSpec(memory_space=pltpu.HBM)
    vmem = pl.BlockSpec(memory_space=pltpu.VMEM)
    shape = (4 * TILE, piece[1] * LANES)
    return pl.pallas_call(
        lambda *refs: first_kernel(piece, *refs),
        out_shape=jax.ShapeDtypeStruct(shape, jnp.bfloat16),
        in_specs=[hbm, hbm],
        out_specs=vmem,
        scratch_shapes=[
            pltpu.VMEM((128, LANES), jnp.float32),
            pltpu.VMEM(shape, jnp.int32),
            pltpu.VMEM((high - low, 128), jnp.float32),
            pltpu.SemaphoreType.DMA((4,)),
            pltpu.SemaphoreType.DMA,
        ],
        compiler_params=pltpu.CompilerParams(vmem_limit_bytes=VMEM_LIMIT),
        name="first_rows",
    )(codes, scales_t)


def dequantize_kernel(parts, codes_ref, scales_ref, *rest):
    *outs, scales = rest
    low, high = block_range([piece for piece, _ in parts])
    scales[:, : high - low] = scales_ref[low:high].T
    for (piece, first), out in zip(parts, outs):
        for j, tail in enumerate(ORDER):
            row = block_row(piece, (first,) + tail)
            dequantize_rows(
                piece,
                row,
                (scales[pl.ds(row, TILE), :], low),
                lambda k: codes_ref[pl.ds(row, TILE), pl.ds((piece[0] + k) * LANES, LANES)],
                out.at[j * TILE : (j + 1) * TILE],
            )


def dequantize(parts, codes, scales):
    vmem = pl.BlockSpec(memory_space=pltpu.VMEM)
    return pl.pallas_call(
        lambda *refs: dequantize_kernel(parts, *refs),
        out_shape=[jax.ShapeDtypeStruct((4 * TILE, piece[1] * LANES), jnp.bfloat16) for piece, _ in parts],
        in_specs=[vmem, vmem],
        out_specs=[vmem for _ in parts],
        scratch_shapes=[pltpu.VMEM((128, LANES), jnp.float32)],
        compiler_params=pltpu.CompilerParams(vmem_limit_bytes=VMEM_LIMIT),
        name="dequantize",
    )(codes, scales)


def finish_kernel(pieces, counts, requant_ref, *refs):
    parts, (send_ref, keep_ref, rows) = refs[: sum(counts)], refs[-3:]
    numerators = requant_ref[...].astype(jnp.float32)
    scale = numerators * (1.0 / 32.0)
    inverse = 32.0 / numerators
    start, blocks = pieces[0][0], sum(piece[1] for piece in pieces)
    stride = rows.shape[0] // (TILE + 1)
    for n, piece in enumerate(pieces):
        arrays = parts[sum(counts[:n]) : sum(counts[: n + 1])]
        for k in range(piece[1]):
            cut = pl.ds(k * LANES, LANES)
            at = piece[0] + k
            partial = arrays[0][arrays[0].shape[0] - TILE :, cut].astype(jnp.float32)
            for array in arrays[1:]:
                partial = partial + array[array.shape[0] - TILE :, cut].astype(jnp.float32)
            coded = jnp.clip(partial * inverse[:, at : at + 1], -8.0, 8.0).astype(jnp.bfloat16)
            rows[pl.ds(at - start, TILE, stride=stride), :] = coded.astype(jnp.float32) * scale[:, at : at + 1]
    wide = lax.axis_index("wide")
    core = wide & 1
    for slot, y_flip in enumerate(Y_FLIPS):
        for z_slot, z_flip in enumerate((1, 0)):
            for ref, owner in ((send_ref, 1 - core), (keep_ref, core)):
                row = pl.multiple_of(wide_at(wide, z_flip, y_flip, owner) * stride, 8)
                ref[slot, z_slot] = rows[pl.ds(row, blocks), :].astype(ref.dtype)


def finish(requant, pieces, parts):
    vmem = pl.BlockSpec(memory_space=pltpu.VMEM)
    blocks = sum(piece[1] for piece in pieces)
    shape = (4, 2, blocks, LANES)
    counts = [len(arrays) for arrays in parts]
    inputs = [requant, *[array for arrays in parts for array in arrays]]
    return pl.pallas_call(
        lambda *refs: finish_kernel(pieces, counts, *refs),
        out_shape=[jax.ShapeDtypeStruct(shape, jnp.bfloat16), jax.ShapeDtypeStruct(shape, jnp.float32)],
        in_specs=[vmem] * len(inputs),
        out_specs=[vmem, vmem],
        scratch_shapes=[pltpu.VMEM(((TILE + 1) * pl.cdiv(blocks, 8) * 8, LANES), jnp.float32)],
        compiler_params=pltpu.CompilerParams(vmem_limit_bytes=VMEM_LIMIT),
        name="finish",
    )(*inputs)


def adamw(gradient, params, first_moment, second_moment, step_count):
    steps = step_count[0].astype(jnp.float32)
    first = decay_first * first_moment + (1.0 - decay_first) * gradient
    second = decay_second * second_moment + (1.0 - decay_second) * gradient * gradient
    bias_first = 1.0 - jnp.power(jnp.float32(decay_first), steps)
    bias_second = 1.0 - jnp.power(jnp.float32(decay_second), steps)
    update = first / bias_first / (jnp.sqrt(second / bias_second) + epsilon) + weight_decay * params
    return (update, first, second)


def send(array, axes, route):
    return lax.ppermute(array.astype(jnp.bfloat16), axes, route)


def total(*arrays):
    result = arrays[0].astype(jnp.float32)
    for array in arrays[1:]:
        result = result + array.astype(jnp.float32)
    return result


def shards(grad_codes, code_scales, requant_scales, params, first_moment, second_moment, step_count):
    codes = pltpu.with_memory_space_constraint(grad_codes, pltpu.HBM)
    scales = code_scales.T
    scales_hbm = pltpu.with_memory_space_constraint(scales, pltpu.HBM)
    firsts = []
    for n, piece in enumerate(PIECES):
        if n == FIRST:
            rows = first_rows(piece, codes, scales_hbm)
        else:
            (rows,) = dequantize([(piece, 1)], grad_codes, scales)
        firsts.append(send(rows, AXES, pairs(piece, 0)))
    keeps = dequantize([(piece, 0) for piece in PIECES], grad_codes, scales)
    parts = [[keep, first] for keep, first in zip(keeps, firsts)]
    last = None
    for n, step in SUMS:
        if last is not None:
            parts[n][step], last = lax.optimization_barrier((parts[n][step], last))
        cut = slice(0, 2 * TILE) if step == 1 else slice(2 * TILE, 3 * TILE)
        last = total(*[array[cut] for array in parts[n][:2]], *[array[:TILE] for array in parts[n][2:]])
        last = last.astype(jnp.bfloat16)
        parts[n].append(send(last, AXES, pairs(PIECES[n], step)))
    other_core = [(b, b ^ 1) for b in range(16)]
    requant = requant_scales.reshape(TILE, BLOCKS)
    near = []
    for cut in (slice(0, EARLY), slice(EARLY, None)):
        away, keep = finish(requant, PIECES[cut], parts[cut])
        requant, away = lax.optimization_barrier((requant, away))
        near.append(total(keep, send(away, "wide", [(b, b ^ 1) for b in range(16)])))
    near = jnp.concatenate(near, axis=2)
    routes = [[(b, wide_at(b, 0, y_flip, b & 1)) for b in range(16)] for y_flip in Y_FLIPS[:3]]
    chip = total(near[3], *[send(near[slot], "wide", route) for slot, route in enumerate(routes)])
    gradient = total(chip[1], send(chip[0], "wide", [(b, b ^ 8) for b in range(16)]))
    tall = (BLOCKS, LANES)
    outs = adamw(gradient, params.reshape(tall), first_moment.reshape(tall), second_moment.reshape(tall), step_count)
    return tuple(out.reshape(1, COLUMNS) for out in outs)


def solution(mesh):
    in_specs = (
        P(("node", "wide"), None),
        P(("node", "wide"), None),
        P("node", "wide", None, None),
        P(("node", "wide"), None),
        P(("node", "wide"), None),
        P(("node", "wide"), None),
        P(),
    )
    out_specs = (P(("node", "wide"), None), P(("node", "wide"), None), P(("node", "wide"), None))
    return jax.shard_map(shards, mesh=mesh, in_specs=in_specs, out_specs=out_specs, check_vma=False)
```

```python
import itertools

import jax
import jax.numpy as jnp
from jax import lax
from jax.experimental import pallas as pl
from jax.experimental.pallas import tpu as pltpu
from jax.sharding import PartitionSpec as P

decay_first = 0.9
decay_second = 0.95
epsilon = 1e-08
weight_decay = 0.1

BLOCKS = 96
LANES = 128
COLUMNS = BLOCKS * LANES
TILE = 16
PIECES = (
    (0, 34, "PZQ"),
    (34, 32, "ZQP"),
    (66, 30, "QPZ"),
)
SUMS = ((0, 1), (1, 1), (2, 1), (0, 2), (1, 2), (2, 2))
EARLY = 1
FIRST = 0
AXES = ("node", "wide")
VMEM_LIMIT = 32 * 1024 * 1024


def bits(node):
    high = node >> 2
    return {"P": ((node >> 1) & 1) ^ high, "Q": high, "Z": node & 1}


def node_of(label):
    return (label["Q"] << 2) | ((label["P"] ^ label["Q"]) << 1) | label["Z"]


Y_FLIPS = ((3, 1, 2, 0), (1, 2, 3, 0))


def wide_at(wide, z_flip, y_flip, core):
    high = ((wide >> 2) & 1) ^ (y_flip >> 1)
    low = (((wide >> 1) ^ (wide >> 2)) & 1) ^ (y_flip & 1)
    return ((wide >> 3) ^ z_flip) << 3 | high << 2 | (high ^ low) << 1 | core


def pairs(piece, *steps):
    result = []
    for node in range(8):
        for wide in range(16):
            label = bits(node)
            for step in steps:
                label[piece[2][step]] ^= 1
            result.append((node * 16 + wide, node_of(label) * 16 + wide))
    return result


def block_row(piece, relative):
    mine = bits(lax.axis_index("node"))
    label = {dim: mine[dim] ^ relative[piece[2].index(dim)] for dim in "PQZ"}
    return pl.multiple_of(node_of(label) * TILE, TILE)


ORDER = ((1, 1), (1, 0), (0, 1), (0, 0))


def block_range(pieces):
    return pieces[0][0] // 8 * 8, pl.cdiv(pieces[-1][0] + pieces[-1][1], 8) * 8


def dequantize_rows(piece, row, scale, codes, out):
    for k in range(piece[1]):
        at = piece[0] + k - scale[1]
        values = (codes(k).astype(jnp.float32) + 0.5) * scale[0][:, at : at + 1]
        out[:, k * LANES : (k + 1) * LANES] = values.astype(jnp.bfloat16)


def first_kernel(piece, codes_ref, scales_ref, out_ref, scales, stage, scales_buf, sem, scale_sem):
    low, high = block_range([piece])
    scale_copy = pltpu.make_async_copy(scales_ref.at[low:high], scales_buf, scale_sem)
    scale_copy.start()
    copies = []
    for j, tail in enumerate(ORDER):
        row = block_row(piece, (1,) + tail)
        copy = pltpu.make_async_copy(
            codes_ref.at[pl.ds(row, TILE), pl.ds(piece[0] * LANES, piece[1] * LANES)],
            stage.at[pl.ds(j * TILE, TILE), :],
            sem.at[j],
        )
        copy.start()
        copies.append((row, copy))
    scale_copy.wait()
    scales[:, : high - low] = scales_buf[...].T
    for j, (row, copy) in enumerate(copies):
        copy.wait()
        rows = slice(j * TILE, (j + 1) * TILE)
        dequantize_rows(
            piece,
            row,
            (scales[pl.ds(row, TILE), :], low),
            lambda k: stage[rows, k * LANES : (k + 1) * LANES],
            out_ref.at[rows],
        )


def first_rows(piece, codes, scales_t):
    low, high = block_range([piece])
    hbm = pl.BlockSpec(memory_space=pltpu.HBM)
    vmem = pl.BlockSpec(memory_space=pltpu.VMEM)
    shape = (4 * TILE, piece[1] * LANES)
    return pl.pallas_call(
        lambda *refs: first_kernel(piece, *refs),
        out_shape=jax.ShapeDtypeStruct(shape, jnp.bfloat16),
        in_specs=[hbm, hbm],
        out_specs=vmem,
        scratch_shapes=[
            pltpu.VMEM((128, LANES), jnp.float32),
            pltpu.VMEM(shape, jnp.int32),
            pltpu.VMEM((high - low, 128), jnp.float32),
            pltpu.SemaphoreType.DMA((4,)),
            pltpu.SemaphoreType.DMA,
        ],
        compiler_params=pltpu.CompilerParams(vmem_limit_bytes=VMEM_LIMIT),
        name="first_rows",
    )(codes, scales_t)


def dequantize_kernel(parts, codes_ref, scales_ref, *rest):
    *outs, scales = rest
    low, high = block_range([piece for piece, _ in parts])
    scales[:, : high - low] = scales_ref[low:high].T
    for (piece, first), out in zip(parts, outs):
        for j, tail in enumerate(ORDER):
            row = block_row(piece, (first,) + tail)
            dequantize_rows(
                piece,
                row,
                (scales[pl.ds(row, TILE), :], low),
                lambda k: codes_ref[pl.ds(row, TILE), pl.ds((piece[0] + k) * LANES, LANES)],
                out.at[j * TILE : (j + 1) * TILE],
            )


def dequantize(parts, codes, scales):
    vmem = pl.BlockSpec(memory_space=pltpu.VMEM)
    return pl.pallas_call(
        lambda *refs: dequantize_kernel(parts, *refs),
        out_shape=[jax.ShapeDtypeStruct((4 * TILE, piece[1] * LANES), jnp.bfloat16) for piece, _ in parts],
        in_specs=[vmem, vmem],
        out_specs=[vmem for _ in parts],
        scratch_shapes=[pltpu.VMEM((128, LANES), jnp.float32)],
        compiler_params=pltpu.CompilerParams(vmem_limit_bytes=VMEM_LIMIT),
        name="dequantize",
    )(codes, scales)


def finish_kernel(pieces, counts, requant_ref, *refs):
    parts, (send_ref, keep_ref, rows) = refs[: sum(counts)], refs[-3:]
    numerators = requant_ref[...].astype(jnp.float32)
    scale = numerators * (1.0 / 32.0)
    inverse = 32.0 / numerators
    start, blocks = pieces[0][0], sum(piece[1] for piece in pieces)
    stride = rows.shape[0] // (TILE + 1)
    for n, piece in enumerate(pieces):
        arrays = parts[sum(counts[:n]) : sum(counts[: n + 1])]
        for k in range(piece[1]):
            cut = pl.ds(k * LANES, LANES)
            at = piece[0] + k
            partial = arrays[0][arrays[0].shape[0] - TILE :, cut].astype(jnp.float32)
            for array in arrays[1:]:
                partial = partial + array[array.shape[0] - TILE :, cut].astype(jnp.float32)
            coded = jnp.clip(partial * inverse[:, at : at + 1], -8.0, 8.0).astype(jnp.bfloat16)
            rows[pl.ds(at - start, TILE, stride=stride), :] = coded.astype(jnp.float32) * scale[:, at : at + 1]
    wide = lax.axis_index("wide")
    core = wide & 1
    for slot, (first, second) in enumerate(zip(*Y_FLIPS)):
        for z_slot, z_flip in enumerate((1, 0)):
            for ref, owner in ((send_ref, 1 - core), (keep_ref, core)):
                y_flip = first + owner * (second - first)
                row = pl.multiple_of(wide_at(wide, z_flip, y_flip, owner) * stride, 8)
                ref[slot, z_slot] = rows[pl.ds(row, blocks), :].astype(ref.dtype)


def finish(requant, pieces, parts):
    vmem = pl.BlockSpec(memory_space=pltpu.VMEM)
    blocks = sum(piece[1] for piece in pieces)
    shape = (4, 2, blocks, LANES)
    counts = [len(arrays) for arrays in parts]
    inputs = [requant, *[array for arrays in parts for array in arrays]]
    return pl.pallas_call(
        lambda *refs: finish_kernel(pieces, counts, *refs),
        out_shape=[jax.ShapeDtypeStruct(shape, jnp.bfloat16), jax.ShapeDtypeStruct(shape, jnp.float32)],
        in_specs=[vmem] * len(inputs),
        out_specs=[vmem, vmem],
        scratch_shapes=[pltpu.VMEM(((TILE + 1) * pl.cdiv(blocks, 8) * 8, LANES), jnp.float32)],
        compiler_params=pltpu.CompilerParams(vmem_limit_bytes=VMEM_LIMIT),
        name="finish",
    )(*inputs)


def adamw(gradient, params, first_moment, second_moment, step_count):
    steps = step_count[0].astype(jnp.float32)
    first = decay_first * first_moment + (1.0 - decay_first) * gradient
    second = decay_second * second_moment + (1.0 - decay_second) * gradient * gradient
    bias_first = 1.0 - jnp.power(jnp.float32(decay_first), steps)
    bias_second = 1.0 - jnp.power(jnp.float32(decay_second), steps)
    update = first / bias_first / (jnp.sqrt(second / bias_second) + epsilon) + weight_decay * params
    return (update, first, second)


def send(array, axes, route):
    return lax.ppermute(array.astype(jnp.bfloat16), axes, route)


def total(*arrays):
    result = arrays[0].astype(jnp.float32)
    for array in arrays[1:]:
        result = result + array.astype(jnp.float32)
    return result


def shards(grad_codes, code_scales, requant_scales, params, first_moment, second_moment, step_count):
    codes = pltpu.with_memory_space_constraint(grad_codes, pltpu.HBM)
    scales = code_scales.T
    scales_hbm = pltpu.with_memory_space_constraint(scales, pltpu.HBM)
    firsts = []
    for n, piece in enumerate(PIECES):
        if n == FIRST:
            rows = first_rows(piece, codes, scales_hbm)
        else:
            (rows,) = dequantize([(piece, 1)], grad_codes, scales)
        firsts.append(send(rows, AXES, pairs(piece, 0)))
    keeps = dequantize([(piece, 0) for piece in PIECES], grad_codes, scales)
    parts = [[keep, first] for keep, first in zip(keeps, firsts)]
    last = None
    for n, step in SUMS:
        if last is not None:
            parts[n][step], last = lax.optimization_barrier((parts[n][step], last))
        cut = slice(0, 2 * TILE) if step == 1 else slice(2 * TILE, 3 * TILE)
        last = total(*[array[cut] for array in parts[n][:2]], *[array[:TILE] for array in parts[n][2:]])
        last = last.astype(jnp.bfloat16)
        parts[n].append(send(last, AXES, pairs(PIECES[n], step)))
    other_core = [(b, b ^ 1) for b in range(16)]
    requant = requant_scales.reshape(TILE, BLOCKS)
    near = []
    for cut in (slice(0, EARLY), slice(EARLY, None)):
        away, keep = finish(requant, PIECES[cut], parts[cut])
        requant, away = lax.optimization_barrier((requant, away))
        near.append(total(keep, send(away, "wide", [(b, b ^ 1) for b in range(16)])))
    near = jnp.concatenate(near, axis=2)
    routes = [[(b, wide_at(b, 0, Y_FLIPS[b & 1][slot], b & 1)) for b in range(16)] for slot in range(3)]
    chip = total(near[3], *[send(near[slot], "wide", route) for slot, route in enumerate(routes)])
    gradient = total(chip[1], send(chip[0], "wide", [(b, b ^ 8) for b in range(16)]))
    tall = (BLOCKS, LANES)
    outs = adamw(gradient, params.reshape(tall), first_moment.reshape(tall), second_moment.reshape(tall), step_count)
    return tuple(out.reshape(1, COLUMNS) for out in outs)


def solution(mesh):
    in_specs = (
        P(("node", "wide"), None),
        P(("node", "wide"), None),
        P("node", "wide", None, None),
        P(("node", "wide"), None),
        P(("node", "wide"), None),
        P(("node", "wide"), None),
        P(),
    )
    out_specs = (P(("node", "wide"), None), P(("node", "wide"), None), P(("node", "wide"), None))
    return jax.shard_map(shards, mesh=mesh, in_specs=in_specs, out_specs=out_specs, check_vma=False)
```

```python
import itertools

import jax
import jax.numpy as jnp
from jax import lax
from jax.experimental import pallas as pl
from jax.experimental.pallas import tpu as pltpu
from jax.sharding import PartitionSpec as P

decay_first = 0.9
decay_second = 0.95
epsilon = 1e-08
weight_decay = 0.1

BLOCKS = 96
LANES = 128
COLUMNS = BLOCKS * LANES
TILE = 16
PIECES = (
    (0, 28, "PZQ"),
    (28, 26, "ZQP"),
    (54, 24, "QPZ"),
    (78, 18, "PQZ"),
)
SUMS = ((0, 1), (1, 1), (2, 1), (3, 1), (0, 2), (1, 2), (2, 2), (3, 2))
EARLY = 2
FIRST = 0
AXES = ("node", "wide")
VMEM_LIMIT = 32 * 1024 * 1024


def bits(node):
    high = node >> 2
    return {"P": ((node >> 1) & 1) ^ high, "Q": high, "Z": node & 1}


def node_of(label):
    return (label["Q"] << 2) | ((label["P"] ^ label["Q"]) << 1) | label["Z"]


Y_FLIPS = ((3, 1, 2, 0), (1, 2, 3, 0))


def wide_at(wide, z_flip, y_flip, core):
    high = ((wide >> 2) & 1) ^ (y_flip >> 1)
    low = (((wide >> 1) ^ (wide >> 2)) & 1) ^ (y_flip & 1)
    return ((wide >> 3) ^ z_flip) << 3 | high << 2 | (high ^ low) << 1 | core


def pairs(piece, *steps):
    result = []
    for node in range(8):
        for wide in range(16):
            label = bits(node)
            for step in steps:
                label[piece[2][step]] ^= 1
            result.append((node * 16 + wide, node_of(label) * 16 + wide))
    return result


def block_row(piece, relative):
    mine = bits(lax.axis_index("node"))
    label = {dim: mine[dim] ^ relative[piece[2].index(dim)] for dim in "PQZ"}
    return pl.multiple_of(node_of(label) * TILE, TILE)


ORDER = ((1, 1), (1, 0), (0, 1), (0, 0))


def block_range(pieces):
    return pieces[0][0] // 8 * 8, pl.cdiv(pieces[-1][0] + pieces[-1][1], 8) * 8


def dequantize_rows(piece, row, scale, codes, out):
    for k in range(piece[1]):
        at = piece[0] + k - scale[1]
        values = (codes(k).astype(jnp.float32) + 0.5) * scale[0][:, at : at + 1]
        out[:, k * LANES : (k + 1) * LANES] = values.astype(jnp.bfloat16)


def first_kernel(piece, codes_ref, scales_ref, out_ref, scales, stage, scales_buf, sem, scale_sem):
    low, high = block_range([piece])
    scale_copy = pltpu.make_async_copy(scales_ref.at[low:high], scales_buf, scale_sem)
    scale_copy.start()
    copies = []
    for j, tail in enumerate(ORDER):
        row = block_row(piece, (1,) + tail)
        copy = pltpu.make_async_copy(
            codes_ref.at[pl.ds(row, TILE), pl.ds(piece[0] * LANES, piece[1] * LANES)],
            stage.at[pl.ds(j * TILE, TILE), :],
            sem.at[j],
        )
        copy.start()
        copies.append((row, copy))
    scale_copy.wait()
    scales[:, : high - low] = scales_buf[...].T
    for j, (row, copy) in enumerate(copies):
        copy.wait()
        rows = slice(j * TILE, (j + 1) * TILE)
        dequantize_rows(
            piece,
            row,
            (scales[pl.ds(row, TILE), :], low),
            lambda k: stage[rows, k * LANES : (k + 1) * LANES],
            out_ref.at[rows],
        )


def first_rows(piece, codes, scales_t):
    low, high = block_range([piece])
    hbm = pl.BlockSpec(memory_space=pltpu.HBM)
    vmem = pl.BlockSpec(memory_space=pltpu.VMEM)
    shape = (4 * TILE, piece[1] * LANES)
    return pl.pallas_call(
        lambda *refs: first_kernel(piece, *refs),
        out_shape=jax.ShapeDtypeStruct(shape, jnp.bfloat16),
        in_specs=[hbm, hbm],
        out_specs=vmem,
        scratch_shapes=[
            pltpu.VMEM((128, LANES), jnp.float32),
            pltpu.VMEM(shape, jnp.int32),
            pltpu.VMEM((high - low, 128), jnp.float32),
            pltpu.SemaphoreType.DMA((4,)),
            pltpu.SemaphoreType.DMA,
        ],
        compiler_params=pltpu.CompilerParams(vmem_limit_bytes=VMEM_LIMIT),
        name="first_rows",
    )(codes, scales_t)


def dequantize_kernel(parts, codes_ref, scales_ref, *rest):
    *outs, scales = rest
    low, high = block_range([piece for piece, _ in parts])
    scales[:, : high - low] = scales_ref[low:high].T
    for (piece, first), out in zip(parts, outs):
        for j, tail in enumerate(ORDER):
            row = block_row(piece, (first,) + tail)
            dequantize_rows(
                piece,
                row,
                (scales[pl.ds(row, TILE), :], low),
                lambda k: codes_ref[pl.ds(row, TILE), pl.ds((piece[0] + k) * LANES, LANES)],
                out.at[j * TILE : (j + 1) * TILE],
            )


def dequantize(parts, codes, scales):
    vmem = pl.BlockSpec(memory_space=pltpu.VMEM)
    return pl.pallas_call(
        lambda *refs: dequantize_kernel(parts, *refs),
        out_shape=[jax.ShapeDtypeStruct((4 * TILE, piece[1] * LANES), jnp.bfloat16) for piece, _ in parts],
        in_specs=[vmem, vmem],
        out_specs=[vmem for _ in parts],
        scratch_shapes=[pltpu.VMEM((128, LANES), jnp.float32)],
        compiler_params=pltpu.CompilerParams(vmem_limit_bytes=VMEM_LIMIT),
        name="dequantize",
    )(codes, scales)


def finish_kernel(pieces, counts, requant_ref, *refs):
    parts, (send_ref, keep_ref, rows) = refs[: sum(counts)], refs[-3:]
    numerators = requant_ref[...].astype(jnp.float32)
    scale = numerators * (1.0 / 32.0)
    inverse = 32.0 / numerators
    start, blocks = pieces[0][0], sum(piece[1] for piece in pieces)
    stride = rows.shape[0] // (TILE + 1)
    for n, piece in enumerate(pieces):
        arrays = parts[sum(counts[:n]) : sum(counts[: n + 1])]
        for k in range(piece[1]):
            cut = pl.ds(k * LANES, LANES)
            at = piece[0] + k
            partial = arrays[0][arrays[0].shape[0] - TILE :, cut].astype(jnp.float32)
            for array in arrays[1:]:
                partial = partial + array[array.shape[0] - TILE :, cut].astype(jnp.float32)
            coded = jnp.clip(partial * inverse[:, at : at + 1], -8.0, 8.0).astype(jnp.bfloat16)
            rows[pl.ds(at - start, TILE, stride=stride), :] = coded.astype(jnp.float32) * scale[:, at : at + 1]
    wide = lax.axis_index("wide")
    core = wide & 1
    for slot, (first, second) in enumerate(zip(*Y_FLIPS)):
        for z_slot, z_flip in enumerate((1, 0)):
            for ref, owner in ((send_ref, 1 - core), (keep_ref, core)):
                y_flip = first + owner * (second - first)
                row = pl.multiple_of(wide_at(wide, z_flip, y_flip, owner) * stride, 8)
                ref[slot, z_slot] = rows[pl.ds(row, blocks), :].astype(ref.dtype)


def finish(requant, pieces, parts):
    vmem = pl.BlockSpec(memory_space=pltpu.VMEM)
    blocks = sum(piece[1] for piece in pieces)
    shape = (4, 2, blocks, LANES)
    counts = [len(arrays) for arrays in parts]
    inputs = [requant, *[array for arrays in parts for array in arrays]]
    return pl.pallas_call(
        lambda *refs: finish_kernel(pieces, counts, *refs),
        out_shape=[jax.ShapeDtypeStruct(shape, jnp.bfloat16), jax.ShapeDtypeStruct(shape, jnp.float32)],
        in_specs=[vmem] * len(inputs),
        out_specs=[vmem, vmem],
        scratch_shapes=[pltpu.VMEM(((TILE + 1) * pl.cdiv(blocks, 8) * 8, LANES), jnp.float32)],
        compiler_params=pltpu.CompilerParams(vmem_limit_bytes=VMEM_LIMIT),
        name="finish",
    )(*inputs)


def adamw(gradient, params, first_moment, second_moment, step_count):
    steps = step_count[0].astype(jnp.float32)
    first = decay_first * first_moment + (1.0 - decay_first) * gradient
    second = decay_second * second_moment + (1.0 - decay_second) * gradient * gradient
    bias_first = 1.0 - jnp.power(jnp.float32(decay_first), steps)
    bias_second = 1.0 - jnp.power(jnp.float32(decay_second), steps)
    update = first / bias_first / (jnp.sqrt(second / bias_second) + epsilon) + weight_decay * params
    return (update, first, second)


def send(array, axes, route):
    return lax.ppermute(array.astype(jnp.bfloat16), axes, route)


def total(*arrays):
    result = arrays[0].astype(jnp.float32)
    for array in arrays[1:]:
        result = result + array.astype(jnp.float32)
    return result


def shards(grad_codes, code_scales, requant_scales, params, first_moment, second_moment, step_count):
    codes = pltpu.with_memory_space_constraint(grad_codes, pltpu.HBM)
    scales = code_scales.T
    scales_hbm = pltpu.with_memory_space_constraint(scales, pltpu.HBM)
    firsts = []
    for n, piece in enumerate(PIECES):
        if n == FIRST:
            rows = first_rows(piece, codes, scales_hbm)
        else:
            (rows,) = dequantize([(piece, 1)], grad_codes, scales)
        firsts.append(send(rows, AXES, pairs(piece, 0)))
    keeps = dequantize([(piece, 0) for piece in PIECES], grad_codes, scales)
    parts = [[keep, first] for keep, first in zip(keeps, firsts)]
    last = None
    for n, step in SUMS:
        if last is not None:
            parts[n][step], last = lax.optimization_barrier((parts[n][step], last))
        cut = slice(0, 2 * TILE) if step == 1 else slice(2 * TILE, 3 * TILE)
        last = total(*[array[cut] for array in parts[n][:2]], *[array[:TILE] for array in parts[n][2:]])
        last = last.astype(jnp.bfloat16)
        parts[n].append(send(last, AXES, pairs(PIECES[n], step)))
    other_core = [(b, b ^ 1) for b in range(16)]
    requant = requant_scales.reshape(TILE, BLOCKS)
    near = []
    for cut in (slice(0, EARLY), slice(EARLY, None)):
        away, keep = finish(requant, PIECES[cut], parts[cut])
        requant, away = lax.optimization_barrier((requant, away))
        near.append(total(keep, send(away, "wide", [(b, b ^ 1) for b in range(16)])))
    near = jnp.concatenate(near, axis=2)
    routes = [[(b, wide_at(b, 0, Y_FLIPS[b & 1][slot], b & 1)) for b in range(16)] for slot in range(3)]
    chip = total(near[3], *[send(near[slot], "wide", route) for slot, route in enumerate(routes)])
    gradient = total(chip[1], send(chip[0], "wide", [(b, b ^ 8) for b in range(16)]))
    tall = (BLOCKS, LANES)
    outs = adamw(gradient, params.reshape(tall), first_moment.reshape(tall), second_moment.reshape(tall), step_count)
    return tuple(out.reshape(1, COLUMNS) for out in outs)


def solution(mesh):
    in_specs = (
        P(("node", "wide"), None),
        P(("node", "wide"), None),
        P("node", "wide", None, None),
        P(("node", "wide"), None),
        P(("node", "wide"), None),
        P(("node", "wide"), None),
        P(),
    )
    out_specs = (P(("node", "wide"), None), P(("node", "wide"), None), P(("node", "wide"), None))
    return jax.shard_map(shards, mesh=mesh, in_specs=in_specs, out_specs=out_specs, check_vma=False)
```
